32 devices in a mesh: bend: 2 (over core), head: 4 (over z), blk: 4 (over y, x).
Axes of the slice: x: 2, y: 2, z: 4, core: 2. Of those that a mesh axis runs over, the one named last changes fastest.
Arguments:
- queries: bfloat16 [4096, 1024], P(('bend', 'head', 'blk')), parts along dimension 0, may hold values from -6 to 6
- keys_in: bfloat16 [4096, 1024], P(('bend', 'head', 'blk')), parts along dimension 0, may hold values from -6 to 6
- values: bfloat16 [4096, 1024], P(('bend', 'head', 'blk')), parts along dimension 0, may hold values from -6 to 6
- d_out: bfloat16 [4096, 1024], P(('bend', 'head', 'blk')), parts along dimension 0, may hold values from -6 to 6
- token_count: int32 [2], P('bend'), parts along dimension 0, may hold values from 1024 to 2048
- block_ids: int32 [32], P('bend'), parts along dimension 0, may hold values from 0 to 15, each once
- neighbours: int32 [32, 10], P('bend'), parts along dimension 0, may hold values from 0 to 15, as said below
Outputs:
- grad_queries: bfloat16 [4096, 1024], P(('bend', 'head', 'blk')), parts along dimension 0
- grad_keys: bfloat16 [4096, 1024], P(('bend', 'head', 'blk')), parts along dimension 0
- grad_values: bfloat16 [4096, 1024], P(('bend', 'head', 'blk')), parts along dimension 0
The draws below stay inside these ranges and needn't reach their ends.
There are 2 independent parts, one for each index of `bend`. The reference program is written for one: setup_inputs(seed, part) draws one part's arguments, and reference() takes and returns one part's arrays. A program takes and returns all parts, laid end to end along the dimension named above; each array names one. Nothing has to cross between parts.
Inputs may be any that keep to these rules, and one draw needn't show every extreme that they name: `neighbours`: column 0 of a row is the query block itself; the 10 entries of a row are distinct; every block appears in exactly 10 rows.
All inputs are finite; a program needn't handle non-finite values.
Results may differ from the reference program's by a relative error of at most 0.017.
Values may be sent and summed in bfloat16 or wider, within the bound.
A program may use at most 128 MiB of HBM per device.

```python
import math
import jax
import jax.numpy as jnp
from jax import lax

H = 16
HD = 64
D = 1024
BLK = 128
NBR = 10
TOKENS = 2048
NBLK = 16


def draw_queries(key, part):
    sample = jnp.clip(jax.random.normal(jax.random.fold_in(key, 11), (TOKENS, D), jnp.float32), -6.0, 6.0)
    return sample.astype(jnp.bfloat16)


def draw_keys_in(key, part):
    sample = jnp.clip(jax.random.normal(jax.random.fold_in(key, 12), (TOKENS, D), jnp.float32), -6.0, 6.0)
    return sample.astype(jnp.bfloat16)


def draw_neighbours(key, part):
    count_blocks = TOKENS // BLK
    row_ids = jnp.arange(count_blocks, dtype=jnp.int32)
    relabel = jax.random.permutation(jax.random.fold_in(key, 31), count_blocks).astype(jnp.int32)
    inverse = jnp.argsort(relabel, stable=True).astype(jnp.int32)
    shifts = (1 + jax.random.permutation(jax.random.fold_in(key, 32), count_blocks - 1)[:NBR - 1]).astype(jnp.int32)
    moved = (relabel[:, None] + shifts[None, :]) % count_blocks
    others = inverse[moved].astype(jnp.int32)
    return jnp.concatenate([row_ids[:, None], others], axis=1).astype(jnp.int32)


def steps_of(stream_key, extent, cuts, low, high):
    level, own = 1.0, jax.random.fold_in(stream_key, 6)
    for dim, parts in cuts:
        draws = jnp.exp(jax.random.uniform(jax.random.fold_in(own, dim), (parts,), jnp.float32, low / len(cuts), high / len(cuts)))
        level = level * jnp.repeat(draws, extent[dim] // parts).reshape([-1 if axis == dim else 1 for axis in range(len(extent))])
    return level


def bell_draw(stream_key, shape, width, limit, cuts=(), held_as=jnp.bfloat16):
    result = jax.random.normal(stream_key, shape, jnp.float32) * width
    if len(cuts) > 0:
        result = steps_of(stream_key, shape, cuts, -0.22, 0.18) * result
    return jnp.clip(result, min=-limit, max=limit).astype(held_as)


def setup_inputs(seed: int = 0, part: int = 0) -> dict:
    keys = jax.random.split(jax.random.key(seed), 8)
    part_keys = jax.random.split(jax.random.fold_in(keys[7], part), 8)
    queries = draw_queries(jax.random.fold_in(jax.random.fold_in(keys[7], part), 71), part)
    keys_in = draw_keys_in(jax.random.fold_in(jax.random.fold_in(keys[7], part), 71), part)
    values = bell_draw(part_keys[2], (TOKENS, D), 1.0, 6.0, ((0, 16),))
    d_out = bell_draw(part_keys[3], (TOKENS, D), 1.0, 6.0, ((0, 16),))
    token_count = jax.random.randint(part_keys[4], (1,), TOKENS // 2, TOKENS + 1).astype(jnp.int32)
    block_ids = jax.random.permutation(part_keys[5], NBLK).astype(jnp.int32)
    neighbours = draw_neighbours(jax.random.fold_in(jax.random.fold_in(keys[7], part), 71), part)
    return {"queries": queries, "keys_in": keys_in, "values": values, "d_out": d_out, "token_count": token_count, "block_ids": block_ids, "neighbours": neighbours}


neg_fill = -1e+30

def reference(queries, keys_in, values, d_out, token_count, block_ids, neighbours):
    count_blocks = TOKENS // BLK
    score_scale = 1.0 / math.sqrt(HD)
    highest = lax.Precision.HIGHEST
    table_ids = jnp.arange(count_blocks, dtype=jnp.int32)
    matches = block_ids[None, :] == table_ids[:, None]
    stored_of = lax.optimization_barrier(jnp.sum(jnp.where(matches, table_ids[None, :], 0), axis=1)).astype(jnp.int32)
    token_limit = token_count[0]
    offsets = jnp.arange(BLK, dtype=jnp.int32)
    row_where = (block_ids[:, None] * BLK + offsets[None, :]).reshape(-1)
    grad_rows = jnp.where((row_where < token_limit)[:, None], d_out, jnp.zeros_like(d_out))
    query_blocks = queries.reshape(count_blocks, BLK, H, HD)
    key_blocks = keys_in.reshape(count_blocks, BLK, H, HD)
    value_blocks = values.reshape(count_blocks, BLK, H, HD)
    grad_blocks = grad_rows.reshape(count_blocks, BLK, H, HD)
    zero_acc = jnp.zeros((count_blocks, BLK, H, HD), jnp.float32)

    def visit_block(running, stored):
        key_sum, value_sum = running
        global_id = block_ids[stored]
        near_global = neighbours[global_id].astype(jnp.int32)
        near_stored = stored_of[near_global].astype(jnp.int32)
        query_where = global_id * BLK + offsets
        key_where = near_global[:, None] * BLK + offsets[None, :]
        allowed = (key_where < token_limit)[None] | (key_where[None] == query_where[:, None, None])
        permit = allowed[None]
        query_tile = query_blocks[stored].astype(jnp.float32)
        grad_tile = grad_blocks[stored].astype(jnp.float32)
        key_tile = key_blocks[near_stored].astype(jnp.float32)
        value_tile = value_blocks[near_stored].astype(jnp.float32)
        product = jnp.einsum('qhd,jkhd->hqjk', query_tile, key_tile, precision=highest) * score_scale
        largest = lax.optimization_barrier(jnp.max(jnp.where(permit, product, neg_fill), axis=(2, 3), keepdims=True))
        denominator = lax.optimization_barrier(jnp.sum(jnp.where(permit, jnp.exp(product - largest), 0.0), axis=(2, 3), keepdims=True))
        log_total = largest + jnp.log(denominator)
        probability = jnp.where(permit, jnp.exp(product - log_total), 0.0)
        grad_probs = jnp.einsum('qhd,jkhd->hqjk', grad_tile, value_tile, precision=highest)
        row_delta = lax.optimization_barrier(jnp.sum(probability * grad_probs, axis=(2, 3), keepdims=True))
        prob_low = probability.astype(jnp.bfloat16)
        grad_scores = (probability * (grad_probs - row_delta)).astype(jnp.bfloat16)
        grad_wide = grad_scores.astype(jnp.float32)
        query_grad = (jnp.einsum('hqjk,jkhd->qhd', grad_wide, key_tile, precision=highest) * score_scale).astype(jnp.bfloat16)
        key_part = jnp.einsum('hqjk,qhd->jkhd', grad_wide, query_tile, precision=highest) * score_scale
        value_part = jnp.einsum('hqjk,qhd->jkhd', prob_low.astype(jnp.float32), grad_tile, precision=highest)
        key_sum = key_sum.at[near_stored].add(key_part)
        value_sum = value_sum.at[near_stored].add(value_part)
        return ((key_sum, value_sum), query_grad)
    (key_sum, value_sum), query_grads = lax.scan(visit_block, (zero_acc, zero_acc), table_ids)
    return (query_grads.reshape(TOKENS, D), key_sum.reshape(TOKENS, D).astype(jnp.bfloat16), value_sum.reshape(TOKENS, D).astype(jnp.bfloat16))
```

```python
import functools
import math

import jax
import jax.numpy as jnp
from jax import lax
from jax.experimental import pallas as pl
from jax.experimental.pallas import tpu as pltpu
from jax.sharding import PartitionSpec as P

HD = 64
BLK = 128


neg_fill = -1e30
row_target = 512


def lookup(entries, wanted):
    matches = wanted[..., None] == jnp.arange(entries.shape[0], dtype=jnp.int32)
    return jnp.sum(jnp.where(matches, entries, 0), axis=-1)


def lookup_rows(entries, wanted):
    matches = wanted[..., None] == jnp.arange(entries.shape[0], dtype=jnp.int32)
    return jnp.sum(jnp.where(matches[..., None], entries, 0), axis=-2)


def group_size(blocks, block_rows):
    target = max(1, min(blocks, row_target // block_rows))
    while blocks % target != 0:
        target = target - 1
    return target


def block_tables(block_ids, neighbours, blk_count, head_count, block_rows, shard_rows):
    per_shard = shard_rows // block_rows
    local_blocks = head_count * per_shard
    slot_ids = jnp.arange(blk_count * local_blocks, dtype=jnp.int32)
    source = slot_ids // local_blocks
    within = slot_ids % local_blocks
    stored = (within // per_shard * blk_count + source) * per_shard + within % per_shard
    global_slot = lookup(block_ids, stored)
    matches = global_slot[None, :] == slot_ids[:, None]
    slot_global = jnp.sum(jnp.where(matches, slot_ids[None, :], 0), axis=1)
    key_global = lookup_rows(neighbours, global_slot)
    key_slots = lookup(slot_global, key_global)
    offsets = jnp.arange(block_rows, dtype=jnp.int32)
    query_where = global_slot[:, None] * block_rows + offsets
    key_where = key_global[:, :, None] * block_rows + offsets
    return (key_slots, query_where, key_where)


def permitted(query_where, key_where, token_limit):
    inside = key_where[:, None] < token_limit
    itself = key_where[:, None] == query_where[:, :, None, None]
    return inside | itself


def head_masks(feature_width, head_width):
    heads_here = feature_width // head_width
    owner_head = jnp.arange(feature_width, dtype=jnp.int32) // head_width
    return owner_head[None, :] == jnp.arange(heads_here, dtype=jnp.int32)[:, None]


def attend_all(query_tile, key_tile, value_tile, grad_tile, allowed, masks, score_scale):
    heads_here = masks.shape[0]
    query_sum = jnp.zeros(query_tile.shape, jnp.float32)
    key_sum = jnp.zeros(key_tile.shape, jnp.float32)
    value_sum = jnp.zeros(key_tile.shape, jnp.float32)
    logs = []
    deltas = []
    for head in range(heads_here):
        column_mask = masks[head]
        query_head = jnp.where(column_mask, query_tile, jnp.zeros_like(query_tile))
        grad_head = jnp.where(column_mask, grad_tile, jnp.zeros_like(grad_tile))
        product = (
            jnp.einsum("gqf,gnkf->gqnk", query_head, key_tile, preferred_element_type=jnp.float32)
            * score_scale
        )
        largest = jnp.max(jnp.where(allowed, product, neg_fill), axis=(2, 3), keepdims=True)
        denominator = jnp.sum(
            jnp.where(allowed, jnp.exp(product - largest), 0.0), axis=(2, 3), keepdims=True
        )
        log_total = largest + jnp.log(denominator)
        probability = jnp.where(allowed, jnp.exp(product - log_total), 0.0)
        grad_probs = jnp.einsum(
            "gqf,gnkf->gqnk", grad_head, value_tile, preferred_element_type=jnp.float32
        )
        row_delta = jnp.sum(probability * grad_probs, axis=(2, 3), keepdims=True)
        grad_scores = (probability * (grad_probs - row_delta)).astype(jnp.bfloat16)
        prob_low = probability.astype(jnp.bfloat16)
        query_term = (
            jnp.einsum("gqnk,gnkf->gqf", grad_scores, key_tile, preferred_element_type=jnp.float32)
            * score_scale
        )
        query_sum = query_sum + jnp.where(column_mask, query_term, 0.0)
        key_sum = (
            key_sum
            + jnp.einsum(
                "gqnk,gqf->gnkf", grad_scores, query_head, preferred_element_type=jnp.float32
            )
            * score_scale
        )
        value_sum = value_sum + jnp.einsum(
            "gqnk,gqf->gnkf", prob_low, grad_head, preferred_element_type=jnp.float32
        )
        logs.append(log_total[:, :, 0, 0])
        deltas.append(row_delta[:, :, 0, 0])
    return (query_sum, key_sum, value_sum, jnp.stack(logs, axis=1), jnp.stack(deltas, axis=1))


def per_device(queries, keys_in, values, d_out, token_count, block_ids, neighbours):
    head_count = lax.axis_size("head")
    blk_count = lax.axis_size("blk")
    blk_index = lax.axis_index("blk")
    shard_rows = queries.shape[0]
    block_rows = BLK
    head_width = HD
    score_scale = 1.0 / math.sqrt(head_width)
    query_rows, key_rows, value_rows, grad_rows = (
        lax.all_to_all(queries, "head", split_axis=1, concat_axis=0, tiled=True),
        lax.all_to_all(keys_in, "head", split_axis=1, concat_axis=0, tiled=True),
        lax.all_to_all(values, "head", split_axis=1, concat_axis=0, tiled=True),
        lax.all_to_all(d_out, "head", split_axis=1, concat_axis=0, tiled=True),
    )
    feature_width = query_rows.shape[1]
    masks = head_masks(feature_width, head_width)
    local_blocks = query_rows.shape[0] // block_rows
    key_slots, query_where, key_where = block_tables(
        block_ids, neighbours, blk_count, head_count, block_rows, shard_rows
    )
    token_limit = token_count[0]
    first_slot = blk_index * local_blocks
    my_key_slots = lax.dynamic_slice_in_dim(key_slots, first_slot, local_blocks, 0)
    my_query_where = lax.dynamic_slice_in_dim(query_where, first_slot, local_blocks, 0)
    my_key_where = lax.dynamic_slice_in_dim(key_where, first_slot, local_blocks, 0)
    row_valid = (my_query_where < token_limit).reshape(-1, 1)
    grad_rows = jnp.where(row_valid, grad_rows, jnp.zeros_like(grad_rows))
    query_blocks = query_rows.reshape(local_blocks, block_rows, feature_width)
    grad_blocks = grad_rows.reshape(local_blocks, block_rows, feature_width)
    gathered_keys, gathered_values = (
        lax.all_gather(key_rows, "blk", axis=0, tiled=True),
        lax.all_gather(value_rows, "blk", axis=0, tiled=True),
    )
    key_blocks = gathered_keys.reshape(-1, block_rows, feature_width)
    value_blocks = gathered_values.reshape(-1, block_rows, feature_width)
    group_blocks = group_size(local_blocks, block_rows)
    steps_count = local_blocks // group_blocks

    def local_tiles(start_block):
        query_tile = lax.dynamic_slice_in_dim(query_blocks, start_block, group_blocks, 0)
        grad_tile = lax.dynamic_slice_in_dim(grad_blocks, start_block, group_blocks, 0)
        slot_tile = lax.dynamic_slice_in_dim(my_key_slots, start_block, group_blocks, 0)
        key_tile = jnp.take(key_blocks, slot_tile, axis=0)
        value_tile = jnp.take(value_blocks, slot_tile, axis=0)
        allowed = permitted(
            lax.dynamic_slice_in_dim(my_query_where, start_block, group_blocks, 0),
            lax.dynamic_slice_in_dim(my_key_where, start_block, group_blocks, 0),
            token_limit,
        )
        return (query_tile, grad_tile, slot_tile, key_tile, value_tile, allowed)

    def summed_step(running, step_index):
        query_tile, grad_tile, slot_tile, key_tile, value_tile, allowed = local_tiles(
            step_index * group_blocks
        )
        query_part, key_part, value_part, log_total, row_delta = attend_all(
            query_tile, key_tile, value_tile, grad_tile, allowed, masks, score_scale
        )
        flat_slots = slot_tile.reshape(-1)
        key_sum = running[0].at[flat_slots].add(key_part.reshape(-1, block_rows, feature_width))
        value_sum = running[1].at[flat_slots].add(value_part.reshape(-1, block_rows, feature_width))
        return ((key_sum, value_sum), query_part)

    zero_acc = jnp.zeros((key_blocks.shape[0], block_rows, feature_width), jnp.float32)
    (key_sum, value_sum), query_parts = lax.scan(
        summed_step, (zero_acc, zero_acc), jnp.arange(steps_count, dtype=jnp.int32)
    )
    key_mine, value_mine = (
        lax.psum_scatter(
            key_sum.astype(jnp.bfloat16), "blk", scatter_dimension=0, tiled=True
        ).astype(jnp.float32),
        lax.psum_scatter(
            value_sum.astype(jnp.bfloat16), "blk", scatter_dimension=0, tiled=True
        ).astype(jnp.float32),
    )
    query_grad_rows = query_parts.reshape(local_blocks * block_rows, feature_width).astype(
        jnp.bfloat16
    )
    key_grad_rows = key_mine.reshape(local_blocks * block_rows, feature_width).astype(jnp.bfloat16)
    value_grad_rows = value_mine.reshape(local_blocks * block_rows, feature_width).astype(
        jnp.bfloat16
    )
    gradients = (
        lax.all_to_all(query_grad_rows, "head", split_axis=0, concat_axis=1, tiled=True),
        lax.all_to_all(key_grad_rows, "head", split_axis=0, concat_axis=1, tiled=True),
        lax.all_to_all(value_grad_rows, "head", split_axis=0, concat_axis=1, tiled=True),
    )
    return (gradients[0], gradients[1], gradients[2])


def head_kernel(
    ring,
    blk_count,
    near,
    limit_ref,
    ids_ref,
    nbr_ref,
    q_ref,
    k_ref,
    v_ref,
    g_ref,
    gq_out,
    gk_out,
    gv_out,
    qk_send,
    gv_send,
    qk_land,
    gv_land,
    kt_buf,
    work,
    prob_wide,
    prob_low,
    dscores,
    out_send,
    out_land,
    stored_of,
    slot_of,
    term_at,
    send_sem,
    recv_sem,
):
    rows = BLK
    width = HD
    scale = 1.0 / math.sqrt(width)
    me = lax.axis_index("head") * blk_count + lax.axis_index("blk")
    limit = limit_ref[0]

    def place(peer):
        return {"head": lax.div(peer, blk_count), "blk": lax.rem(peer, blk_count)}

    def copy_to(kind, source, target, slot, peer):
        return pltpu.make_async_remote_copy(
            src_ref=source,
            dst_ref=target,
            send_sem=send_sem.at[kind, slot],
            recv_sem=recv_sem.at[kind, me],
            device_id=place(peer),
            device_id_type=pl.DeviceIdType.MESH,
        )

    def await_from(kind, target, peer):
        pltpu.make_async_remote_copy(
            src_ref=target,
            dst_ref=target,
            send_sem=send_sem.at[kind, peer],
            recv_sem=recv_sem.at[kind, peer],
            device_id=place(peer),
            device_id_type=pl.DeviceIdType.MESH,
        ).wait_recv()

    def others(body):
        def step(distance, carry):
            body(lax.rem(me + distance, ring))
            return carry

        lax.fori_loop(1, ring, step, 0)

    barrier = pltpu.get_barrier_semaphore()
    others(
        lambda peer: pl.semaphore_signal(
            barrier, inc=1, device_id=place(peer), device_id_type=pl.DeviceIdType.MESH
        )
    )

    row_index = lax.broadcasted_iota(jnp.int32, (rows, 2 * width), 0)

    my_limit = limit - ids_ref[me] * rows
    for pair in range(ring // 2):
        columns = slice(pair * 2 * width, (pair + 1) * 2 * width)
        q_tile = q_ref[:, columns] * jnp.asarray(scale, jnp.bfloat16)
        k_tile = k_ref[:, columns]
        g_tile = jnp.where(row_index < my_limit, g_ref[:, columns].astype(jnp.float32), 0.0)
        g_tile = g_tile.astype(jnp.bfloat16)
        v_tile = v_ref[:, columns]
        for side in range(2):
            part = slice(side * width, (side + 1) * width)
            qk_send[2 * pair + side] = jnp.concatenate([q_tile[:, part], k_tile[:, part]], axis=1)
            gv_send[2 * pair + side] = jnp.concatenate([g_tile[:, part], v_tile[:, part]], axis=1)

    pl.semaphore_wait(barrier, ring - 1)
    others(lambda peer: copy_to(0, qk_send.at[peer], qk_land.at[me], peer, peer).start())
    others(lambda peer: copy_to(1, gv_send.at[peer], gv_land.at[me], peer, peer).start())
    qk_land[me] = qk_send[me]
    gv_land[me] = gv_send[me]

    def find_stored(block, carry):
        where = jnp.int32(0)
        for stored in range(ring):
            where = jnp.where(ids_ref[stored] == block, jnp.int32(stored), where)
        stored_of[block] = where
        return carry

    lax.fori_loop(0, ring, find_stored, 0)

    def find_slots(query, carry):
        block = ids_ref[query]
        for entry in range(near):
            slot_of[query * near + entry] = stored_of[nbr_ref[block, entry]]
        return carry

    lax.fori_loop(0, ring, find_slots, 0)

    def find_terms(key, carry):
        def visit(query, state):
            count, found = state[0], state[1:]
            hit = jnp.int32(-1)
            for entry in range(near):
                term = query * near + entry
                hit = jnp.where(slot_of[term] == key, term, hit)
            found = tuple(
                jnp.where((count == rank) & (hit >= 0), hit, found[rank]) for rank in range(near)
            )
            return (jnp.where(hit >= 0, count + 1, count),) + found

        state = lax.fori_loop(0, ring, visit, (jnp.int32(0),) * (near + 1))
        for rank in range(near):
            term_at[key * near + rank] = state[rank + 1]
        return carry

    lax.fori_loop(0, ring, find_terms, 0)

    others(lambda peer: await_from(0, qk_land.at[peer], peer))

    def turn_keys(block, carry):
        tile = qk_land[block].astype(jnp.float32)
        kt_buf[block] = tile.T[width:, :].astype(jnp.bfloat16)
        return carry

    lax.fori_loop(0, ring, turn_keys, 0)

    nt = (((1,), (1,)), ((), ()))
    upper = lax.broadcasted_iota(jnp.int32, (rows, 2 * width), 1) >= width

    def as_upper(tile):
        wide = tile.astype(jnp.float32)
        moved = jnp.concatenate([wide[:, width:], wide[:, :width]], axis=1)
        return jnp.where(upper, moved, 0.0).astype(jnp.bfloat16)

    itself = row_index == lax.broadcasted_iota(jnp.int32, (rows, rows), 1)

    def allowed(block, entry):
        real = row_index < limit - nbr_ref[block, entry] * rows
        return real | itself if entry == 0 else real

    def weigh(query, carry):
        block = ids_ref[query]
        against = as_upper(qk_land[query])
        keys = jnp.concatenate(
            [qk_land[slot_of[query * near + entry]] for entry in range(near)], axis=0
        )
        scores = lax.dot_general(keys, against, nt, preferred_element_type=jnp.float32)
        scores = jnp.concatenate(
            [
                jnp.where(
                    allowed(block, entry),
                    scores[entry * rows : (entry + 1) * rows],
                    neg_fill,
                )
                for entry in range(near)
            ],
            axis=0,
        )
        work[...] = scores
        largest = jnp.max(scores, axis=0, keepdims=True)
        grown = jnp.exp(work[...] - largest)
        prob_wide[query] = grown
        shrink = 1.0 / jnp.sum(grown, axis=0, keepdims=True)
        prob = prob_wide[query] * shrink
        prob_wide[query] = prob
        prob_low[pl.ds(query * near, near)] = prob.astype(jnp.bfloat16).reshape(near, rows, rows)
        return carry

    lax.fori_loop(0, ring, weigh, 0)

    def hand_out(kind, block, tile):
        out_send[kind, block] = tile

        @pl.when(block != me)
        def _():
            copy_to(
                2 + kind, out_send.at[kind, block], out_land.at[kind, me], block, block
            ).start()

        @pl.when(block == me)
        def _():
            out_land[kind, me] = tile

    def fold(tile):
        return jnp.concatenate([tile[: rows // 2, :width], tile[rows // 2 :, :width]], axis=1)

    def key_terms(kind, weights, tiles):
        def one(key, carry):
            terms = [term_at[key * near + rank] for rank in range(near)]
            left = jnp.concatenate([weights[term] for term in terms], axis=1)
            right = jnp.concatenate([tiles[lax.div(term, near)] for term in terms], axis=0)
            total = jnp.dot(left, right, preferred_element_type=jnp.float32)
            hand_out(kind, key, fold(total).astype(jnp.bfloat16))
            return carry

        lax.fori_loop(0, ring, one, 0)

    others(lambda peer: await_from(1, gv_land.at[peer], peer))
    key_terms(2, prob_low, gv_land)

    def differentiate(query, carry):
        against = as_upper(gv_land[query])
        slots = [slot_of[query * near + entry] for entry in range(near)]
        values = jnp.concatenate([gv_land[slot] for slot in slots], axis=0)
        work[...] = lax.dot_general(values, against, nt, preferred_element_type=jnp.float32)
        delta = jnp.sum(prob_wide[query] * work[...], axis=0, keepdims=True)
        slope = (prob_wide[query] * (work[...] - delta)).astype(jnp.bfloat16)
        dscores[pl.ds(query * near, near)] = slope.reshape(near, rows, rows)
        turned = jnp.concatenate([kt_buf[slot] for slot in slots], axis=1)
        total = jnp.dot(turned, slope, preferred_element_type=jnp.float32) * scale
        hand_out(0, query, total.astype(jnp.bfloat16))
        return carry

    lax.fori_loop(0, ring, differentiate, 0)
    key_terms(1, dscores, qk_land)

    def unfold(kind, out):
        for pair in range(ring // 2):
            columns = slice(pair * 2 * width, (pair + 1) * 2 * width)
            first, second = out_land[kind, 2 * pair], out_land[kind, 2 * pair + 1]
            out[: rows // 2, columns] = jnp.concatenate(
                [first[:, :width], second[:, :width]], axis=1
            )
            out[rows // 2 :, columns] = jnp.concatenate(
                [first[:, width:], second[:, width:]], axis=1
            )

    others(lambda peer: await_from(4, out_land.at[2, peer], peer))
    unfold(2, gv_out)
    others(lambda peer: await_from(2, out_land.at[0, peer], peer))
    for pair in range(ring // 2):
        columns = slice(pair * 2 * width, (pair + 1) * 2 * width)
        tile = jnp.concatenate([out_land[0, 2 * pair], out_land[0, 2 * pair + 1]], axis=0)
        gq_out[:, columns] = tile.astype(jnp.float32).T.astype(jnp.bfloat16)
    others(lambda peer: await_from(3, out_land.at[1, peer], peer))
    unfold(1, gk_out)

    others(lambda peer: copy_to(0, qk_send.at[peer], qk_land.at[me], peer, peer).wait_send())
    others(lambda peer: copy_to(1, gv_send.at[peer], gv_land.at[me], peer, peer).wait_send())
    for kind in range(3):
        others(
            lambda peer: copy_to(
                2 + kind, out_send.at[kind, peer], out_land.at[kind, me], peer, peer
            ).wait_send()
        )


def per_head_device(
    ring, blk_count, queries, keys_in, values, d_out, token_count, block_ids, neighbours
):
    rows, features = queries.shape
    near = neighbours.shape[1]
    tile = (rows, 2 * HD)
    low = jnp.bfloat16
    smem = pl.BlockSpec(memory_space=pltpu.SMEM)
    vmem = pl.BlockSpec(memory_space=pltpu.VMEM)
    return pl.pallas_call(
        functools.partial(head_kernel, ring, blk_count, near),
        out_shape=[jax.ShapeDtypeStruct((rows, features), low)] * 3,
        in_specs=[smem] * 3 + [vmem] * 4,
        out_specs=[vmem] * 3,
        scratch_shapes=[
            pltpu.VMEM((ring,) + tile, low),
            pltpu.VMEM((ring,) + tile, low),
            pltpu.VMEM((ring,) + tile, low),
            pltpu.VMEM((ring,) + tile, low),
            pltpu.VMEM((ring, HD, rows), low),
            pltpu.VMEM((near * rows, rows), jnp.float32),
            pltpu.VMEM((ring, near * rows, rows), jnp.float32),
            pltpu.VMEM((ring * near, rows, rows), low),
            pltpu.VMEM((ring * near, rows, rows), low),
            pltpu.VMEM((3, ring, HD, rows), low),
            pltpu.VMEM((3, ring, HD, rows), low),
            pltpu.SMEM((ring,), jnp.int32),
            pltpu.SMEM((ring * near,), jnp.int32),
            pltpu.SMEM((ring * near,), jnp.int32),
            pltpu.SemaphoreType.DMA((5, ring)),
            pltpu.SemaphoreType.DMA((5, ring)),
        ],
        compiler_params=pltpu.CompilerParams(
            collective_id=0, has_side_effects=True, vmem_limit_bytes=48 * 1024 * 1024
        ),
        cost_estimate=pl.CostEstimate(
            flops=10 * ring * near * rows * rows * HD,
            bytes_accessed=14 * rows * features,
            transcendentals=ring * near * rows * rows,
        ),
    )(token_count, block_ids, neighbours, queries, keys_in, values, d_out)


def route(mesh, queries, *rest):
    rows, features = queries.shape
    ring = mesh.shape["head"] * mesh.shape["blk"]
    if rows == BLK and features == ring * HD and 2 * HD == BLK:
        return tuple(per_head_device(ring, mesh.shape["blk"], queries, *rest))
    return per_device(queries, *rest)


def solution(mesh):
    return jax.shard_map(
        functools.partial(route, mesh),
        mesh=mesh,
        in_specs=(
            P(("bend", "head", "blk"), None),
            P(("bend", "head", "blk"), None),
            P(("bend", "head", "blk"), None),
            P(("bend", "head", "blk"), None),
            P("bend"),
            P("bend"),
            P("bend", None),
        ),
        out_specs=(
            P(("bend", "head", "blk"), None),
            P(("bend", "head", "blk"), None),
            P(("bend", "head", "blk"), None),
        ),
        check_vma=False,
    )
```

```python
import functools
import math

import jax
import jax.numpy as jnp
from jax import lax
from jax.experimental import pallas as pl
from jax.experimental.pallas import tpu as pltpu
from jax.sharding import PartitionSpec as P

HD = 64
BLK = 128


neg_fill = -1e30
row_target = 512


def lookup(entries, wanted):
    matches = wanted[..., None] == jnp.arange(entries.shape[0], dtype=jnp.int32)
    return jnp.sum(jnp.where(matches, entries, 0), axis=-1)


def lookup_rows(entries, wanted):
    matches = wanted[..., None] == jnp.arange(entries.shape[0], dtype=jnp.int32)
    return jnp.sum(jnp.where(matches[..., None], entries, 0), axis=-2)


def group_size(blocks, block_rows):
    target = max(1, min(blocks, row_target // block_rows))
    while blocks % target != 0:
        target = target - 1
    return target


def block_tables(block_ids, neighbours, blk_count, head_count, block_rows, shard_rows):
    per_shard = shard_rows // block_rows
    local_blocks = head_count * per_shard
    slot_ids = jnp.arange(blk_count * local_blocks, dtype=jnp.int32)
    source = slot_ids // local_blocks
    within = slot_ids % local_blocks
    stored = (within // per_shard * blk_count + source) * per_shard + within % per_shard
    global_slot = lookup(block_ids, stored)
    matches = global_slot[None, :] == slot_ids[:, None]
    slot_global = jnp.sum(jnp.where(matches, slot_ids[None, :], 0), axis=1)
    key_global = lookup_rows(neighbours, global_slot)
    key_slots = lookup(slot_global, key_global)
    offsets = jnp.arange(block_rows, dtype=jnp.int32)
    query_where = global_slot[:, None] * block_rows + offsets
    key_where = key_global[:, :, None] * block_rows + offsets
    return (key_slots, query_where, key_where)


def permitted(query_where, key_where, token_limit):
    inside = key_where[:, None] < token_limit
    itself = key_where[:, None] == query_where[:, :, None, None]
    return inside | itself


def head_masks(feature_width, head_width):
    heads_here = feature_width // head_width
    owner_head = jnp.arange(feature_width, dtype=jnp.int32) // head_width
    return owner_head[None, :] == jnp.arange(heads_here, dtype=jnp.int32)[:, None]


def attend_all(query_tile, key_tile, value_tile, grad_tile, allowed, masks, score_scale):
    heads_here = masks.shape[0]
    query_sum = jnp.zeros(query_tile.shape, jnp.float32)
    key_sum = jnp.zeros(key_tile.shape, jnp.float32)
    value_sum = jnp.zeros(key_tile.shape, jnp.float32)
    logs = []
    deltas = []
    for head in range(heads_here):
        column_mask = masks[head]
        query_head = jnp.where(column_mask, query_tile, jnp.zeros_like(query_tile))
        grad_head = jnp.where(column_mask, grad_tile, jnp.zeros_like(grad_tile))
        product = (
            jnp.einsum("gqf,gnkf->gqnk", query_head, key_tile, preferred_element_type=jnp.float32)
            * score_scale
        )
        largest = jnp.max(jnp.where(allowed, product, neg_fill), axis=(2, 3), keepdims=True)
        denominator = jnp.sum(
            jnp.where(allowed, jnp.exp(product - largest), 0.0), axis=(2, 3), keepdims=True
        )
        log_total = largest + jnp.log(denominator)
        probability = jnp.where(allowed, jnp.exp(product - log_total), 0.0)
        grad_probs = jnp.einsum(
            "gqf,gnkf->gqnk", grad_head, value_tile, preferred_element_type=jnp.float32
        )
        row_delta = jnp.sum(probability * grad_probs, axis=(2, 3), keepdims=True)
        grad_scores = (probability * (grad_probs - row_delta)).astype(jnp.bfloat16)
        prob_low = probability.astype(jnp.bfloat16)
        query_term = (
            jnp.einsum("gqnk,gnkf->gqf", grad_scores, key_tile, preferred_element_type=jnp.float32)
            * score_scale
        )
        query_sum = query_sum + jnp.where(column_mask, query_term, 0.0)
        key_sum = (
            key_sum
            + jnp.einsum(
                "gqnk,gqf->gnkf", grad_scores, query_head, preferred_element_type=jnp.float32
            )
            * score_scale
        )
        value_sum = value_sum + jnp.einsum(
            "gqnk,gqf->gnkf", prob_low, grad_head, preferred_element_type=jnp.float32
        )
        logs.append(log_total[:, :, 0, 0])
        deltas.append(row_delta[:, :, 0, 0])
    return (query_sum, key_sum, value_sum, jnp.stack(logs, axis=1), jnp.stack(deltas, axis=1))


def per_device(queries, keys_in, values, d_out, token_count, block_ids, neighbours):
    head_count = lax.axis_size("head")
    blk_count = lax.axis_size("blk")
    blk_index = lax.axis_index("blk")
    shard_rows = queries.shape[0]
    block_rows = BLK
    head_width = HD
    score_scale = 1.0 / math.sqrt(head_width)
    query_rows, key_rows, value_rows, grad_rows = (
        lax.all_to_all(queries, "head", split_axis=1, concat_axis=0, tiled=True),
        lax.all_to_all(keys_in, "head", split_axis=1, concat_axis=0, tiled=True),
        lax.all_to_all(values, "head", split_axis=1, concat_axis=0, tiled=True),
        lax.all_to_all(d_out, "head", split_axis=1, concat_axis=0, tiled=True),
    )
    feature_width = query_rows.shape[1]
    masks = head_masks(feature_width, head_width)
    local_blocks = query_rows.shape[0] // block_rows
    key_slots, query_where, key_where = block_tables(
        block_ids, neighbours, blk_count, head_count, block_rows, shard_rows
    )
    token_limit = token_count[0]
    first_slot = blk_index * local_blocks
    my_key_slots = lax.dynamic_slice_in_dim(key_slots, first_slot, local_blocks, 0)
    my_query_where = lax.dynamic_slice_in_dim(query_where, first_slot, local_blocks, 0)
    my_key_where = lax.dynamic_slice_in_dim(key_where, first_slot, local_blocks, 0)
    row_valid = (my_query_where < token_limit).reshape(-1, 1)
    grad_rows = jnp.where(row_valid, grad_rows, jnp.zeros_like(grad_rows))
    query_blocks = query_rows.reshape(local_blocks, block_rows, feature_width)
    grad_blocks = grad_rows.reshape(local_blocks, block_rows, feature_width)
    gathered_keys, gathered_values = (
        lax.all_gather(key_rows, "blk", axis=0, tiled=True),
        lax.all_gather(value_rows, "blk", axis=0, tiled=True),
    )
    key_blocks = gathered_keys.reshape(-1, block_rows, feature_width)
    value_blocks = gathered_values.reshape(-1, block_rows, feature_width)
    group_blocks = group_size(local_blocks, block_rows)
    steps_count = local_blocks // group_blocks

    def local_tiles(start_block):
        query_tile = lax.dynamic_slice_in_dim(query_blocks, start_block, group_blocks, 0)
        grad_tile = lax.dynamic_slice_in_dim(grad_blocks, start_block, group_blocks, 0)
        slot_tile = lax.dynamic_slice_in_dim(my_key_slots, start_block, group_blocks, 0)
        key_tile = jnp.take(key_blocks, slot_tile, axis=0)
        value_tile = jnp.take(value_blocks, slot_tile, axis=0)
        allowed = permitted(
            lax.dynamic_slice_in_dim(my_query_where, start_block, group_blocks, 0),
            lax.dynamic_slice_in_dim(my_key_where, start_block, group_blocks, 0),
            token_limit,
        )
        return (query_tile, grad_tile, slot_tile, key_tile, value_tile, allowed)

    def summed_step(running, step_index):
        query_tile, grad_tile, slot_tile, key_tile, value_tile, allowed = local_tiles(
            step_index * group_blocks
        )
        query_part, key_part, value_part, log_total, row_delta = attend_all(
            query_tile, key_tile, value_tile, grad_tile, allowed, masks, score_scale
        )
        flat_slots = slot_tile.reshape(-1)
        key_sum = running[0].at[flat_slots].add(key_part.reshape(-1, block_rows, feature_width))
        value_sum = running[1].at[flat_slots].add(value_part.reshape(-1, block_rows, feature_width))
        return ((key_sum, value_sum), query_part)

    zero_acc = jnp.zeros((key_blocks.shape[0], block_rows, feature_width), jnp.float32)
    (key_sum, value_sum), query_parts = lax.scan(
        summed_step, (zero_acc, zero_acc), jnp.arange(steps_count, dtype=jnp.int32)
    )
    key_mine, value_mine = (
        lax.psum_scatter(
            key_sum.astype(jnp.bfloat16), "blk", scatter_dimension=0, tiled=True
        ).astype(jnp.float32),
        lax.psum_scatter(
            value_sum.astype(jnp.bfloat16), "blk", scatter_dimension=0, tiled=True
        ).astype(jnp.float32),
    )
    query_grad_rows = query_parts.reshape(local_blocks * block_rows, feature_width).astype(
        jnp.bfloat16
    )
    key_grad_rows = key_mine.reshape(local_blocks * block_rows, feature_width).astype(jnp.bfloat16)
    value_grad_rows = value_mine.reshape(local_blocks * block_rows, feature_width).astype(
        jnp.bfloat16
    )
    gradients = (
        lax.all_to_all(query_grad_rows, "head", split_axis=0, concat_axis=1, tiled=True),
        lax.all_to_all(key_grad_rows, "head", split_axis=0, concat_axis=1, tiled=True),
        lax.all_to_all(value_grad_rows, "head", split_axis=0, concat_axis=1, tiled=True),
    )
    return (gradients[0], gradients[1], gradients[2])


def head_kernel(
    ring,
    blk_count,
    near,
    limit_ref,
    ids_ref,
    nbr_ref,
    q_hbm,
    k_hbm,
    v_hbm,
    g_hbm,
    gq_out,
    gk_out,
    gv_out,
    q_ref,
    k_ref,
    v_ref,
    g_ref,
    qk_send,
    gv_send,
    qk_land,
    gv_land,
    kt_buf,
    work,
    prob_wide,
    prob_low,
    dscores,
    out_send,
    out_land,
    stored_of,
    slot_of,
    term_at,
    load_sem,
    send_sem,
    recv_sem,
):
    rows = BLK
    width = HD
    scale = 1.0 / math.sqrt(width)
    me = lax.axis_index("head") * blk_count + lax.axis_index("blk")
    limit = limit_ref[0]

    def place(peer):
        return {"head": lax.div(peer, blk_count), "blk": lax.rem(peer, blk_count)}

    def copy_to(kind, source, target, slot, peer):
        return pltpu.make_async_remote_copy(
            src_ref=source,
            dst_ref=target,
            send_sem=send_sem.at[kind, slot],
            recv_sem=recv_sem.at[kind, me],
            device_id=place(peer),
            device_id_type=pl.DeviceIdType.MESH,
        )

    def await_from(kind, target, peer):
        pltpu.make_async_remote_copy(
            src_ref=target,
            dst_ref=target,
            send_sem=send_sem.at[kind, peer],
            recv_sem=recv_sem.at[kind, peer],
            device_id=place(peer),
            device_id_type=pl.DeviceIdType.MESH,
        ).wait_recv()

    def others(body):
        def step(distance, carry):
            body(lax.rem(me + distance, ring))
            return carry

        lax.fori_loop(1, ring, step, 0)

    sources = ((q_hbm, q_ref), (k_hbm, k_ref), (g_hbm, g_ref), (v_hbm, v_ref))
    loads = [
        pltpu.make_async_copy(source, held, load_sem.at[index])
        for index, (source, held) in enumerate(sources)
    ]
    for load in loads:
        load.start()

    barrier = pltpu.get_barrier_semaphore()
    others(
        lambda peer: pl.semaphore_signal(
            barrier, inc=1, device_id=place(peer), device_id_type=pl.DeviceIdType.MESH
        )
    )

    row_index = lax.broadcasted_iota(jnp.int32, (rows, 2 * width), 0)

    for load in loads:
        load.wait()
    my_limit = limit - ids_ref[me] * rows
    for pair in range(ring // 2):
        columns = slice(pair * 2 * width, (pair + 1) * 2 * width)
        q_tile = q_ref[:, columns] * jnp.asarray(scale, jnp.bfloat16)
        k_tile = k_ref[:, columns]
        g_tile = jnp.where(row_index < my_limit, g_ref[:, columns].astype(jnp.float32), 0.0)
        g_tile = g_tile.astype(jnp.bfloat16)
        v_tile = v_ref[:, columns]
        for side in range(2):
            part = slice(side * width, (side + 1) * width)
            qk_send[2 * pair + side] = jnp.concatenate([q_tile[:, part], k_tile[:, part]], axis=1)
            gv_send[2 * pair + side] = jnp.concatenate([g_tile[:, part], v_tile[:, part]], axis=1)

    pl.semaphore_wait(barrier, ring - 1)
    others(lambda peer: copy_to(0, qk_send.at[peer], qk_land.at[me], peer, peer).start())
    others(lambda peer: copy_to(1, gv_send.at[peer], gv_land.at[me], peer, peer).start())
    qk_land[me] = qk_send[me]
    gv_land[me] = gv_send[me]

    def find_stored(block, carry):
        where = jnp.int32(0)
        for stored in range(ring):
            where = jnp.where(ids_ref[stored] == block, jnp.int32(stored), where)
        stored_of[block] = where
        return carry

    lax.fori_loop(0, ring, find_stored, 0)

    def find_slots(query, carry):
        block = ids_ref[query]
        for entry in range(near):
            slot_of[query * near + entry] = stored_of[nbr_ref[block, entry]]
        return carry

    lax.fori_loop(0, ring, find_slots, 0)

    def find_terms(key, carry):
        def visit(query, state):
            hit = jnp.int32(-1)
            for entry in range(near):
                term = query * near + entry
                hit = jnp.where(slot_of[term] == key, term, hit)
            return tuple(
                jnp.where(hit >= 0, older, held) for older, held in zip((hit,) + state, state)
            )

        state = lax.fori_loop(0, ring, visit, (jnp.int32(0),) * near)
        for rank in range(near):
            term_at[key * near + rank] = state[rank]
        return carry

    lax.fori_loop(0, ring, find_terms, 0)

    others(lambda peer: await_from(0, qk_land.at[peer], peer))

    def turn_keys(block, carry):
        tile = qk_land[block].astype(jnp.float32)
        kt_buf[block] = tile.T[width:, :].astype(jnp.bfloat16)
        return carry

    lax.fori_loop(0, ring, turn_keys, 0)

    nt = (((1,), (1,)), ((), ()))
    upper = lax.broadcasted_iota(jnp.int32, (rows, 2 * width), 1) >= width

    def as_upper(tile):
        wide = tile.astype(jnp.float32)
        moved = jnp.concatenate([wide[:, width:], wide[:, :width]], axis=1)
        return jnp.where(upper, moved, 0.0).astype(jnp.bfloat16)

    itself = row_index == lax.broadcasted_iota(jnp.int32, (rows, rows), 1)

    def allowed(block, entry):
        real = row_index < limit - nbr_ref[block, entry] * rows
        return real | itself if entry == 0 else real

    def weigh(query, carry):
        block = ids_ref[query]
        against = as_upper(qk_land[query])
        keys = jnp.concatenate(
            [qk_land[slot_of[query * near + entry]] for entry in range(near)], axis=0
        )
        scores = lax.dot_general(keys, against, nt, preferred_element_type=jnp.float32)
        scores = jnp.concatenate(
            [
                jnp.where(
                    allowed(block, entry),
                    scores[entry * rows : (entry + 1) * rows],
                    neg_fill,
                )
                for entry in range(near)
            ],
            axis=0,
        )
        work[...] = scores
        largest = jnp.max(scores, axis=0, keepdims=True)
        grown = jnp.exp(work[...] - largest)
        prob_wide[query] = grown
        shrink = 1.0 / jnp.sum(grown, axis=0, keepdims=True)
        prob = prob_wide[query] * shrink
        prob_wide[query] = prob
        prob_low[pl.ds(query * near, near)] = prob.astype(jnp.bfloat16).reshape(near, rows, rows)
        return carry

    lax.fori_loop(0, ring, weigh, 0)

    def hand_out(kind, block, tile):
        out_send[kind, block] = tile

        @pl.when(block != me)
        def _():
            copy_to(
                2 + kind, out_send.at[kind, block], out_land.at[kind, me], block, block
            ).start()

        @pl.when(block == me)
        def _():
            out_land[kind, me] = tile

    def fold(tile):
        return jnp.concatenate([tile[: rows // 2, :width], tile[rows // 2 :, :width]], axis=1)

    def key_terms(kind, weights, tiles):
        def one(step, carry):
            key = lax.rem(me + 1 + step, ring)
            terms = [term_at[key * near + rank] for rank in range(near)]
            left = jnp.concatenate([weights[term] for term in terms], axis=1)
            right = jnp.concatenate([tiles[lax.div(term, near)] for term in terms], axis=0)
            total = jnp.dot(left, right, preferred_element_type=jnp.float32)
            hand_out(kind, key, fold(total).astype(jnp.bfloat16))
            return carry

        lax.fori_loop(0, ring, one, 0)

    others(lambda peer: await_from(1, gv_land.at[peer], peer))
    key_terms(2, prob_low, gv_land)

    def differentiate(step, carry):
        query = lax.rem(me + 1 + step, ring)
        against = as_upper(gv_land[query])
        slots = [slot_of[query * near + entry] for entry in range(near)]
        values = jnp.concatenate([gv_land[slot] for slot in slots], axis=0)
        work[...] = lax.dot_general(values, against, nt, preferred_element_type=jnp.float32)
        delta = jnp.sum(prob_wide[query] * work[...], axis=0, keepdims=True)
        slope = (prob_wide[query] * (work[...] - delta)).astype(jnp.bfloat16)
        dscores[pl.ds(query * near, near)] = slope.reshape(near, rows, rows)
        turned = jnp.concatenate([kt_buf[slot] for slot in slots], axis=1)
        total = jnp.dot(turned, slope, preferred_element_type=jnp.float32) * scale
        hand_out(0, query, total.astype(jnp.bfloat16))
        return carry

    lax.fori_loop(0, ring, differentiate, 0)
    key_terms(1, dscores, qk_land)

    def unfold(kind, out):
        for pair in range(ring // 2):
            columns = slice(pair * 2 * width, (pair + 1) * 2 * width)
            first, second = out_land[kind, 2 * pair], out_land[kind, 2 * pair + 1]
            out[: rows // 2, columns] = jnp.concatenate(
                [first[:, :width], second[:, :width]], axis=1
            )
            out[rows // 2 :, columns] = jnp.concatenate(
                [first[:, width:], second[:, width:]], axis=1
            )

    others(lambda peer: await_from(4, out_land.at[2, peer], peer))
    unfold(2, gv_out)
    others(lambda peer: await_from(2, out_land.at[0, peer], peer))
    for pair in range(ring // 2):
        columns = slice(pair * 2 * width, (pair + 1) * 2 * width)
        tile = jnp.concatenate([out_land[0, 2 * pair], out_land[0, 2 * pair + 1]], axis=0)
        gq_out[:, columns] = tile.astype(jnp.float32).T.astype(jnp.bfloat16)
    others(lambda peer: await_from(3, out_land.at[1, peer], peer))
    unfold(1, gk_out)

    others(lambda peer: copy_to(0, qk_send.at[peer], qk_land.at[me], peer, peer).wait_send())
    others(lambda peer: copy_to(1, gv_send.at[peer], gv_land.at[me], peer, peer).wait_send())
    for kind in range(3):
        others(
            lambda peer: copy_to(
                2 + kind, out_send.at[kind, peer], out_land.at[kind, me], peer, peer
            ).wait_send()
        )


def per_head_device(
    ring, blk_count, queries, keys_in, values, d_out, token_count, block_ids, neighbours
):
    rows, features = queries.shape
    near = neighbours.shape[1]
    tile = (rows, 2 * HD)
    low = jnp.bfloat16
    smem = pl.BlockSpec(memory_space=pltpu.SMEM)
    vmem = pl.BlockSpec(memory_space=pltpu.VMEM)
    return pl.pallas_call(
        functools.partial(head_kernel, ring, blk_count, near),
        out_shape=[jax.ShapeDtypeStruct((rows, features), low)] * 3,
        in_specs=[smem] * 3 + [pl.BlockSpec(memory_space=pltpu.HBM)] * 4,
        out_specs=[vmem] * 3,
        scratch_shapes=[pltpu.VMEM((rows, features), low)] * 4
        + [
            pltpu.VMEM((ring,) + tile, low),
            pltpu.VMEM((ring,) + tile, low),
            pltpu.VMEM((ring,) + tile, low),
            pltpu.VMEM((ring,) + tile, low),
            pltpu.VMEM((ring, HD, rows), low),
            pltpu.VMEM((near * rows, rows), jnp.float32),
            pltpu.VMEM((ring, near * rows, rows), jnp.float32),
            pltpu.VMEM((ring * near, rows, rows), low),
            pltpu.VMEM((ring * near, rows, rows), low),
            pltpu.VMEM((3, ring, HD, rows), low),
            pltpu.VMEM((3, ring, HD, rows), low),
            pltpu.SMEM((ring,), jnp.int32),
            pltpu.SMEM((ring * near,), jnp.int32),
            pltpu.SMEM((ring * near,), jnp.int32),
            pltpu.SemaphoreType.DMA((4,)),
            pltpu.SemaphoreType.DMA((5, ring)),
            pltpu.SemaphoreType.DMA((5, ring)),
        ],
        compiler_params=pltpu.CompilerParams(
            collective_id=0, has_side_effects=True, vmem_limit_bytes=48 * 1024 * 1024
        ),
        cost_estimate=pl.CostEstimate(
            flops=10 * ring * near * rows * rows * HD,
            bytes_accessed=14 * rows * features,
            transcendentals=ring * near * rows * rows,
        ),
    )(token_count, block_ids, neighbours, queries, keys_in, values, d_out)


def route(mesh, queries, *rest):
    rows, features = queries.shape
    ring = mesh.shape["head"] * mesh.shape["blk"]
    if rows == BLK and features == ring * HD and 2 * HD == BLK:
        return tuple(per_head_device(ring, mesh.shape["blk"], queries, *rest))
    return per_device(queries, *rest)


def solution(mesh):
    return jax.shard_map(
        functools.partial(route, mesh),
        mesh=mesh,
        in_specs=(
            P(("bend", "head", "blk"), None),
            P(("bend", "head", "blk"), None),
            P(("bend", "head", "blk"), None),
            P(("bend", "head", "blk"), None),
            P("bend"),
            P("bend"),
            P("bend", None),
        ),
        out_specs=(
            P(("bend", "head", "blk"), None),
            P(("bend", "head", "blk"), None),
            P(("bend", "head", "blk"), None),
        ),
        check_vma=False,
    )
```

```python
import functools
import math

import jax
import jax.numpy as jnp
from jax import lax
from jax.experimental import pallas as pl
from jax.experimental.pallas import tpu as pltpu
from jax.sharding import PartitionSpec as P

HD = 64
BLK = 128


neg_fill = -1e30
row_target = 512


def lookup(entries, wanted):
    matches = wanted[..., None] == jnp.arange(entries.shape[0], dtype=jnp.int32)
    return jnp.sum(jnp.where(matches, entries, 0), axis=-1)


def lookup_rows(entries, wanted):
    matches = wanted[..., None] == jnp.arange(entries.shape[0], dtype=jnp.int32)
    return jnp.sum(jnp.where(matches[..., None], entries, 0), axis=-2)


def group_size(blocks, block_rows):
    target = max(1, min(blocks, row_target // block_rows))
    while blocks % target != 0:
        target = target - 1
    return target


def block_tables(block_ids, neighbours, blk_count, head_count, block_rows, shard_rows):
    per_shard = shard_rows // block_rows
    local_blocks = head_count * per_shard
    slot_ids = jnp.arange(blk_count * local_blocks, dtype=jnp.int32)
    source = slot_ids // local_blocks
    within = slot_ids % local_blocks
    stored = (within // per_shard * blk_count + source) * per_shard + within % per_shard
    global_slot = lookup(block_ids, stored)
    matches = global_slot[None, :] == slot_ids[:, None]
    slot_global = jnp.sum(jnp.where(matches, slot_ids[None, :], 0), axis=1)
    key_global = lookup_rows(neighbours, global_slot)
    key_slots = lookup(slot_global, key_global)
    offsets = jnp.arange(block_rows, dtype=jnp.int32)
    query_where = global_slot[:, None] * block_rows + offsets
    key_where = key_global[:, :, None] * block_rows + offsets
    return (key_slots, query_where, key_where)


def permitted(query_where, key_where, token_limit):
    inside = key_where[:, None] < token_limit
    itself = key_where[:, None] == query_where[:, :, None, None]
    return inside | itself


def head_masks(feature_width, head_width):
    heads_here = feature_width // head_width
    owner_head = jnp.arange(feature_width, dtype=jnp.int32) // head_width
    return owner_head[None, :] == jnp.arange(heads_here, dtype=jnp.int32)[:, None]


def attend_all(query_tile, key_tile, value_tile, grad_tile, allowed, masks, score_scale):
    heads_here = masks.shape[0]
    query_sum = jnp.zeros(query_tile.shape, jnp.float32)
    key_sum = jnp.zeros(key_tile.shape, jnp.float32)
    value_sum = jnp.zeros(key_tile.shape, jnp.float32)
    logs = []
    deltas = []
    for head in range(heads_here):
        column_mask = masks[head]
        query_head = jnp.where(column_mask, query_tile, jnp.zeros_like(query_tile))
        grad_head = jnp.where(column_mask, grad_tile, jnp.zeros_like(grad_tile))
        product = (
            jnp.einsum("gqf,gnkf->gqnk", query_head, key_tile, preferred_element_type=jnp.float32)
            * score_scale
        )
        largest = jnp.max(jnp.where(allowed, product, neg_fill), axis=(2, 3), keepdims=True)
        denominator = jnp.sum(
            jnp.where(allowed, jnp.exp(product - largest), 0.0), axis=(2, 3), keepdims=True
        )
        log_total = largest + jnp.log(denominator)
        probability = jnp.where(allowed, jnp.exp(product - log_total), 0.0)
        grad_probs = jnp.einsum(
            "gqf,gnkf->gqnk", grad_head, value_tile, preferred_element_type=jnp.float32
        )
        row_delta = jnp.sum(probability * grad_probs, axis=(2, 3), keepdims=True)
        grad_scores = (probability * (grad_probs - row_delta)).astype(jnp.bfloat16)
        prob_low = probability.astype(jnp.bfloat16)
        query_term = (
            jnp.einsum("gqnk,gnkf->gqf", grad_scores, key_tile, preferred_element_type=jnp.float32)
            * score_scale
        )
        query_sum = query_sum + jnp.where(column_mask, query_term, 0.0)
        key_sum = (
            key_sum
            + jnp.einsum(
                "gqnk,gqf->gnkf", grad_scores, query_head, preferred_element_type=jnp.float32
            )
            * score_scale
        )
        value_sum = value_sum + jnp.einsum(
            "gqnk,gqf->gnkf", prob_low, grad_head, preferred_element_type=jnp.float32
        )
        logs.append(log_total[:, :, 0, 0])
        deltas.append(row_delta[:, :, 0, 0])
    return (query_sum, key_sum, value_sum, jnp.stack(logs, axis=1), jnp.stack(deltas, axis=1))


def per_device(queries, keys_in, values, d_out, token_count, block_ids, neighbours):
    head_count = lax.axis_size("head")
    blk_count = lax.axis_size("blk")
    blk_index = lax.axis_index("blk")
    shard_rows = queries.shape[0]
    block_rows = BLK
    head_width = HD
    score_scale = 1.0 / math.sqrt(head_width)
    query_rows, key_rows, value_rows, grad_rows = (
        lax.all_to_all(queries, "head", split_axis=1, concat_axis=0, tiled=True),
        lax.all_to_all(keys_in, "head", split_axis=1, concat_axis=0, tiled=True),
        lax.all_to_all(values, "head", split_axis=1, concat_axis=0, tiled=True),
        lax.all_to_all(d_out, "head", split_axis=1, concat_axis=0, tiled=True),
    )
    feature_width = query_rows.shape[1]
    masks = head_masks(feature_width, head_width)
    local_blocks = query_rows.shape[0] // block_rows
    key_slots, query_where, key_where = block_tables(
        block_ids, neighbours, blk_count, head_count, block_rows, shard_rows
    )
    token_limit = token_count[0]
    first_slot = blk_index * local_blocks
    my_key_slots = lax.dynamic_slice_in_dim(key_slots, first_slot, local_blocks, 0)
    my_query_where = lax.dynamic_slice_in_dim(query_where, first_slot, local_blocks, 0)
    my_key_where = lax.dynamic_slice_in_dim(key_where, first_slot, local_blocks, 0)
    row_valid = (my_query_where < token_limit).reshape(-1, 1)
    grad_rows = jnp.where(row_valid, grad_rows, jnp.zeros_like(grad_rows))
    query_blocks = query_rows.reshape(local_blocks, block_rows, feature_width)
    grad_blocks = grad_rows.reshape(local_blocks, block_rows, feature_width)
    gathered_keys, gathered_values = (
        lax.all_gather(key_rows, "blk", axis=0, tiled=True),
        lax.all_gather(value_rows, "blk", axis=0, tiled=True),
    )
    key_blocks = gathered_keys.reshape(-1, block_rows, feature_width)
    value_blocks = gathered_values.reshape(-1, block_rows, feature_width)
    group_blocks = group_size(local_blocks, block_rows)
    steps_count = local_blocks // group_blocks

    def local_tiles(start_block):
        query_tile = lax.dynamic_slice_in_dim(query_blocks, start_block, group_blocks, 0)
        grad_tile = lax.dynamic_slice_in_dim(grad_blocks, start_block, group_blocks, 0)
        slot_tile = lax.dynamic_slice_in_dim(my_key_slots, start_block, group_blocks, 0)
        key_tile = jnp.take(key_blocks, slot_tile, axis=0)
        value_tile = jnp.take(value_blocks, slot_tile, axis=0)
        allowed = permitted(
            lax.dynamic_slice_in_dim(my_query_where, start_block, group_blocks, 0),
            lax.dynamic_slice_in_dim(my_key_where, start_block, group_blocks, 0),
            token_limit,
        )
        return (query_tile, grad_tile, slot_tile, key_tile, value_tile, allowed)

    def summed_step(running, step_index):
        query_tile, grad_tile, slot_tile, key_tile, value_tile, allowed = local_tiles(
            step_index * group_blocks
        )
        query_part, key_part, value_part, log_total, row_delta = attend_all(
            query_tile, key_tile, value_tile, grad_tile, allowed, masks, score_scale
        )
        flat_slots = slot_tile.reshape(-1)
        key_sum = running[0].at[flat_slots].add(key_part.reshape(-1, block_rows, feature_width))
        value_sum = running[1].at[flat_slots].add(value_part.reshape(-1, block_rows, feature_width))
        return ((key_sum, value_sum), query_part)

    zero_acc = jnp.zeros((key_blocks.shape[0], block_rows, feature_width), jnp.float32)
    (key_sum, value_sum), query_parts = lax.scan(
        summed_step, (zero_acc, zero_acc), jnp.arange(steps_count, dtype=jnp.int32)
    )
    key_mine, value_mine = (
        lax.psum_scatter(
            key_sum.astype(jnp.bfloat16), "blk", scatter_dimension=0, tiled=True
        ).astype(jnp.float32),
        lax.psum_scatter(
            value_sum.astype(jnp.bfloat16), "blk", scatter_dimension=0, tiled=True
        ).astype(jnp.float32),
    )
    query_grad_rows = query_parts.reshape(local_blocks * block_rows, feature_width).astype(
        jnp.bfloat16
    )
    key_grad_rows = key_mine.reshape(local_blocks * block_rows, feature_width).astype(jnp.bfloat16)
    value_grad_rows = value_mine.reshape(local_blocks * block_rows, feature_width).astype(
        jnp.bfloat16
    )
    gradients = (
        lax.all_to_all(query_grad_rows, "head", split_axis=0, concat_axis=1, tiled=True),
        lax.all_to_all(key_grad_rows, "head", split_axis=0, concat_axis=1, tiled=True),
        lax.all_to_all(value_grad_rows, "head", split_axis=0, concat_axis=1, tiled=True),
    )
    return (gradients[0], gradients[1], gradients[2])


def head_kernel(
    ring,
    blk_count,
    near,
    limit_ref,
    ids_ref,
    nbr_ref,
    q_hbm,
    k_hbm,
    v_hbm,
    g_hbm,
    gq_out,
    gk_out,
    gv_out,
    q_ref,
    k_ref,
    v_ref,
    g_ref,
    qk_send,
    gv_send,
    qk_land,
    gv_land,
    kt_buf,
    key_biased,
    work,
    work_next,
    shrink,
    shrink_row,
    prob_low,
    dscores,
    out_send,
    out_land,
    stored_of,
    slot_of,
    term_at,
    load_sem,
    send_sem,
    recv_sem,
):
    rows = BLK
    width = HD
    scale = 1.0 / math.sqrt(width)
    me = lax.axis_index("head") * blk_count + lax.axis_index("blk")
    limit = limit_ref[0]

    def place(peer):
        return {"head": lax.div(peer, blk_count), "blk": lax.rem(peer, blk_count)}

    def copy_to(kind, source, target, slot, peer):
        return pltpu.make_async_remote_copy(
            src_ref=source,
            dst_ref=target,
            send_sem=send_sem.at[kind, slot],
            recv_sem=recv_sem.at[kind, me],
            device_id=place(peer),
            device_id_type=pl.DeviceIdType.MESH,
        )

    def await_from(kind, target, peer):
        pltpu.make_async_remote_copy(
            src_ref=target,
            dst_ref=target,
            send_sem=send_sem.at[kind, peer],
            recv_sem=recv_sem.at[kind, peer],
            device_id=place(peer),
            device_id_type=pl.DeviceIdType.MESH,
        ).wait_recv()

    def others(body):
        def step(distance, carry):
            body(lax.rem(me + distance, ring))
            return carry

        lax.fori_loop(1, ring, step, 0)

    sources = ((q_hbm, q_ref), (k_hbm, k_ref), (g_hbm, g_ref), (v_hbm, v_ref))
    loads = [
        pltpu.make_async_copy(source, held, load_sem.at[index])
        for index, (source, held) in enumerate(sources)
    ]
    for load in loads:
        load.start()

    barrier = pltpu.get_barrier_semaphore()
    others(
        lambda peer: pl.semaphore_signal(
            barrier, inc=1, device_id=place(peer), device_id_type=pl.DeviceIdType.MESH
        )
    )

    row_index = lax.broadcasted_iota(jnp.int32, (rows, 2 * width), 0)

    for load in loads:
        load.wait()
    my_limit = limit - ids_ref[me] * rows
    for pair in range(ring // 2):
        columns = slice(pair * 2 * width, (pair + 1) * 2 * width)
        q_tile = q_ref[:, columns] * jnp.asarray(scale, jnp.bfloat16)
        k_tile = k_ref[:, columns]
        g_tile = jnp.where(row_index < my_limit, g_ref[:, columns].astype(jnp.float32), 0.0)
        g_tile = g_tile.astype(jnp.bfloat16)
        v_tile = v_ref[:, columns]
        for side in range(2):
            part = slice(side * width, (side + 1) * width)
            qk_send[2 * pair + side] = jnp.concatenate([q_tile[:, part], k_tile[:, part]], axis=1)
            gv_send[2 * pair + side] = jnp.concatenate([g_tile[:, part], v_tile[:, part]], axis=1)

    pl.semaphore_wait(barrier, ring - 1)
    others(lambda peer: copy_to(0, qk_send.at[peer], qk_land.at[me], peer, peer).start())
    others(lambda peer: copy_to(1, gv_send.at[peer], gv_land.at[me], peer, peer).start())
    qk_land[me] = qk_send[me]
    gv_land[me] = gv_send[me]

    def find_stored(block, carry):
        where = jnp.int32(0)
        for stored in range(ring):
            where = jnp.where(ids_ref[stored] == block, jnp.int32(stored), where)
        stored_of[block] = where
        return carry

    lax.fori_loop(0, ring, find_stored, 0)

    def find_slots(query, carry):
        block = ids_ref[query]
        for entry in range(near):
            slot_of[query * near + entry] = stored_of[nbr_ref[block, entry]]
        return carry

    lax.fori_loop(0, ring, find_slots, 0)

    def find_terms(key, carry):
        def visit(query, state):
            hit = jnp.int32(-1)
            for entry in range(near):
                term = query * near + entry
                hit = jnp.where(slot_of[term] == key, term, hit)
            return tuple(
                jnp.where(hit >= 0, older, held) for older, held in zip((hit,) + state, state)
            )

        state = lax.fori_loop(0, ring, visit, (jnp.int32(0),) * near)
        for rank in range(near):
            term_at[key * near + rank] = state[rank]
        return carry

    lax.fori_loop(0, ring, find_terms, 0)

    others(lambda peer: await_from(0, qk_land.at[peer], peer))

    lane = lax.broadcasted_iota(jnp.int32, (rows, 2 * width), 1)
    upper = lane >= width

    def turn_keys(block, carry):
        tile = qk_land[block].astype(jnp.float32)
        kt_buf[block] = tile.T[width:, :].astype(jnp.bfloat16)
        real = row_index < limit - ids_ref[block] * rows
        bias = jnp.where((lane == 0) & ~real, neg_fill, 0.0)
        key_biased[block] = jnp.where(upper, tile, bias).astype(jnp.bfloat16)
        return carry

    lax.fori_loop(0, ring, turn_keys, 0)

    nt = (((1,), (1,)), ((), ()))

    def as_upper(tile, lowest):
        wide = tile.astype(jnp.float32)
        moved = jnp.concatenate([wide[:, width:], wide[:, :width]], axis=1)
        return jnp.where(upper, moved, jnp.where(lane == 0, lowest, 0.0)).astype(jnp.bfloat16)

    itself = row_index == lax.broadcasted_iota(jnp.int32, (rows, rows), 1)

    def weigh(query, held):
        block = ids_ref[query]
        own = slot_of[query * near]
        against = as_upper(qk_land[query], 1.0)
        keys = jnp.concatenate(
            [key_biased[slot_of[query * near + entry]] for entry in range(1, near)], axis=0
        )
        first = lax.dot_general(
            qk_land[own], as_upper(qk_land[query], 0.0), nt, preferred_element_type=jnp.float32
        )
        real = row_index < limit - block * rows
        held[:rows] = jnp.where(real | itself, first, neg_fill)
        held[rows:] = lax.dot_general(keys, against, nt, preferred_element_type=jnp.float32)
        largest = jnp.max(held[...], axis=0, keepdims=True)
        grown = jnp.exp(held[...] - largest).astype(jnp.bfloat16)
        total = jnp.sum(grown.astype(jnp.float32), axis=0, keepdims=True)
        prob_low[pl.ds(query * near, near)] = grown.reshape(near, rows, rows)
        shrink[query] = jnp.broadcast_to(1.0 / total, (rows, rows)).T
        shrink_row[query] = jnp.broadcast_to(1.0 / total, (8, rows))

    def weigh_two(step, carry):
        weigh(2 * step, work)
        weigh(2 * step + 1, work_next)
        return carry

    lax.fori_loop(0, ring // 2, weigh_two, 0)

    def hand_out(kind, block, tile):
        out_send[kind, block] = tile

        @pl.when(block != me)
        def _():
            copy_to(
                2 + kind, out_send.at[kind, block], out_land.at[kind, me], block, block
            ).start()

        @pl.when(block == me)
        def _():
            out_land[kind, me] = tile

    def fold(tile):
        return jnp.concatenate([tile[: rows // 2, :width], tile[rows // 2 :, :width]], axis=1)

    def key_terms(weights, tiles, key):
        terms = [term_at[key * near + rank] for rank in range(near)]
        left = jnp.concatenate([weights[term] for term in terms], axis=1)
        right = jnp.concatenate([tiles[lax.div(term, near)] for term in terms], axis=0)
        total = jnp.dot(left, right, preferred_element_type=jnp.float32)
        return fold(total).astype(jnp.bfloat16)

    others(lambda peer: await_from(1, gv_land.at[peer], peer))

    def scale_grads(block, carry):
        tile = gv_land[block].astype(jnp.float32)
        gv_land[block] = jnp.where(upper, tile, tile * shrink[block]).astype(jnp.bfloat16)
        return carry

    lax.fori_loop(0, ring, scale_grads, 0)

    def differentiate(query, held):
        against = as_upper(gv_land[query], 0.0)
        slots = [slot_of[query * near + entry] for entry in range(near)]
        values = jnp.concatenate([gv_land[slot] for slot in slots], axis=0)
        held[...] = lax.dot_general(values, against, nt, preferred_element_type=jnp.float32)
        prob = prob_low[pl.ds(query * near, near)].reshape(near * rows, rows)
        delta = jnp.sum(prob.astype(jnp.float32) * held[...], axis=0, keepdims=True)
        delta = delta * shrink_row[query][:1]
        slope = (prob.astype(jnp.float32) * (held[...] - delta)).astype(jnp.bfloat16)
        dscores[pl.ds(query * near, near)] = slope.reshape(near, rows, rows)
        turned = jnp.concatenate([kt_buf[slot] for slot in slots], axis=1)
        total = jnp.dot(turned, slope, preferred_element_type=jnp.float32) * scale
        return total.astype(jnp.bfloat16)

    def middle(step, carry):
        first = lax.rem(me + 1 + 2 * step, ring)
        second = lax.rem(me + 2 + 2 * step, ring)
        results = (
            (0, first, differentiate(first, work)),
            (2, first, key_terms(prob_low, gv_land, first)),
            (0, second, differentiate(second, work_next)),
            (2, second, key_terms(prob_low, gv_land, second)),
        )
        for result in results:
            hand_out(*result)
        return carry

    lax.fori_loop(0, ring // 2, middle, 0)

    def last(step, carry):
        first = lax.rem(me + 1 + 2 * step, ring)
        second = lax.rem(me + 2 + 2 * step, ring)
        results = (
            (1, first, key_terms(dscores, qk_land, first)),
            (1, second, key_terms(dscores, qk_land, second)),
        )
        for result in results:
            hand_out(*result)
        return carry

    lax.fori_loop(0, ring // 2, last, 0)

    def unfold(kind, out):
        for pair in range(ring // 2):
            columns = slice(pair * 2 * width, (pair + 1) * 2 * width)
            first, second = out_land[kind, 2 * pair], out_land[kind, 2 * pair + 1]
            out[: rows // 2, columns] = jnp.concatenate(
                [first[:, :width], second[:, :width]], axis=1
            )
            out[rows // 2 :, columns] = jnp.concatenate(
                [first[:, width:], second[:, width:]], axis=1
            )

    others(lambda peer: await_from(4, out_land.at[2, peer], peer))
    unfold(2, gv_out)
    others(lambda peer: await_from(2, out_land.at[0, peer], peer))
    for pair in range(ring // 2):
        columns = slice(pair * 2 * width, (pair + 1) * 2 * width)
        tile = jnp.concatenate([out_land[0, 2 * pair], out_land[0, 2 * pair + 1]], axis=0)
        gq_out[:, columns] = tile.astype(jnp.float32).T.astype(jnp.bfloat16)
    others(lambda peer: await_from(3, out_land.at[1, peer], peer))
    unfold(1, gk_out)

    others(lambda peer: copy_to(0, qk_send.at[peer], qk_land.at[me], peer, peer).wait_send())
    others(lambda peer: copy_to(1, gv_send.at[peer], gv_land.at[me], peer, peer).wait_send())
    for kind in range(3):
        others(
            lambda peer: copy_to(
                2 + kind, out_send.at[kind, peer], out_land.at[kind, me], peer, peer
            ).wait_send()
        )


def per_head_device(
    ring, blk_count, queries, keys_in, values, d_out, token_count, block_ids, neighbours
):
    rows, features = queries.shape
    near = neighbours.shape[1]
    tile = (rows, 2 * HD)
    low = jnp.bfloat16
    smem = pl.BlockSpec(memory_space=pltpu.SMEM)
    vmem = pl.BlockSpec(memory_space=pltpu.VMEM)
    return pl.pallas_call(
        functools.partial(head_kernel, ring, blk_count, near),
        out_shape=[jax.ShapeDtypeStruct((rows, features), low)] * 3,
        in_specs=[smem] * 3 + [pl.BlockSpec(memory_space=pl.ANY)] * 4,
        out_specs=[vmem] * 3,
        scratch_shapes=[pltpu.VMEM((rows, features), low)] * 4
        + [
            pltpu.VMEM((ring,) + tile, low),
            pltpu.VMEM((ring,) + tile, low),
            pltpu.VMEM((ring,) + tile, low),
            pltpu.VMEM((ring,) + tile, low),
            pltpu.VMEM((ring, HD, rows), low),
            pltpu.VMEM((ring,) + tile, low),
            pltpu.VMEM((near * rows, rows), jnp.float32),
            pltpu.VMEM((near * rows, rows), jnp.float32),
            pltpu.VMEM((ring, rows, rows), jnp.float32),
            pltpu.VMEM((ring, 8, rows), jnp.float32),
            pltpu.VMEM((ring * near, rows, rows), low),
            pltpu.VMEM((ring * near, rows, rows), low),
            pltpu.VMEM((3, ring, HD, rows), low),
            pltpu.VMEM((3, ring, HD, rows), low),
            pltpu.SMEM((ring,), jnp.int32),
            pltpu.SMEM((ring * near,), jnp.int32),
            pltpu.SMEM((ring * near,), jnp.int32),
            pltpu.SemaphoreType.DMA((4,)),
            pltpu.SemaphoreType.DMA((5, ring)),
            pltpu.SemaphoreType.DMA((5, ring)),
        ],
        compiler_params=pltpu.CompilerParams(
            collective_id=0, has_side_effects=True, vmem_limit_bytes=60 * 1024 * 1024
        ),
        cost_estimate=pl.CostEstimate(
            flops=10 * ring * near * rows * rows * HD,
            bytes_accessed=14 * rows * features,
            transcendentals=ring * near * rows * rows,
        ),
    )(token_count, block_ids, neighbours, queries, keys_in, values, d_out)


def route(mesh, queries, *rest):
    rows, features = queries.shape
    ring = mesh.shape["head"] * mesh.shape["blk"]
    if rows == BLK and features == ring * HD and 2 * HD == BLK and ring % 2 == 0:
        return tuple(per_head_device(ring, mesh.shape["blk"], queries, *rest))
    return per_device(queries, *rest)


def solution(mesh):
    return jax.shard_map(
        functools.partial(route, mesh),
        mesh=mesh,
        in_specs=(
            P(("bend", "head", "blk"), None),
            P(("bend", "head", "blk"), None),
            P(("bend", "head", "blk"), None),
            P(("bend", "head", "blk"), None),
            P("bend"),
            P("bend"),
            P("bend", None),
        ),
        out_specs=(
            P(("bend", "head", "blk"), None),
            P(("bend", "head", "blk"), None),
            P(("bend", "head", "blk"), None),
        ),
        check_vma=False,
    )
```

```python
import functools
import math

import jax
import jax.numpy as jnp
from jax import lax
from jax.experimental import pallas as pl
from jax.experimental.pallas import tpu as pltpu
from jax.sharding import PartitionSpec as P

HD = 64
BLK = 128


neg_fill = -1e30
row_target = 512


def lookup(entries, wanted):
    matches = wanted[..., None] == jnp.arange(entries.shape[0], dtype=jnp.int32)
    return jnp.sum(jnp.where(matches, entries, 0), axis=-1)


def lookup_rows(entries, wanted):
    matches = wanted[..., None] == jnp.arange(entries.shape[0], dtype=jnp.int32)
    return jnp.sum(jnp.where(matches[..., None], entries, 0), axis=-2)


def group_size(blocks, block_rows):
    target = max(1, min(blocks, row_target // block_rows))
    while blocks % target != 0:
        target = target - 1
    return target


def block_tables(block_ids, neighbours, blk_count, head_count, block_rows, shard_rows):
    per_shard = shard_rows // block_rows
    local_blocks = head_count * per_shard
    slot_ids = jnp.arange(blk_count * local_blocks, dtype=jnp.int32)
    source = slot_ids // local_blocks
    within = slot_ids % local_blocks
    stored = (within // per_shard * blk_count + source) * per_shard + within % per_shard
    global_slot = lookup(block_ids, stored)
    matches = global_slot[None, :] == slot_ids[:, None]
    slot_global = jnp.sum(jnp.where(matches, slot_ids[None, :], 0), axis=1)
    key_global = lookup_rows(neighbours, global_slot)
    key_slots = lookup(slot_global, key_global)
    offsets = jnp.arange(block_rows, dtype=jnp.int32)
    query_where = global_slot[:, None] * block_rows + offsets
    key_where = key_global[:, :, None] * block_rows + offsets
    return (key_slots, query_where, key_where)


def permitted(query_where, key_where, token_limit):
    inside = key_where[:, None] < token_limit
    itself = key_where[:, None] == query_where[:, :, None, None]
    return inside | itself


def head_masks(feature_width, head_width):
    heads_here = feature_width // head_width
    owner_head = jnp.arange(feature_width, dtype=jnp.int32) // head_width
    return owner_head[None, :] == jnp.arange(heads_here, dtype=jnp.int32)[:, None]


def attend_all(query_tile, key_tile, value_tile, grad_tile, allowed, masks, score_scale):
    heads_here = masks.shape[0]
    query_sum = jnp.zeros(query_tile.shape, jnp.float32)
    key_sum = jnp.zeros(key_tile.shape, jnp.float32)
    value_sum = jnp.zeros(key_tile.shape, jnp.float32)
    logs = []
    deltas = []
    for head in range(heads_here):
        column_mask = masks[head]
        query_head = jnp.where(column_mask, query_tile, jnp.zeros_like(query_tile))
        grad_head = jnp.where(column_mask, grad_tile, jnp.zeros_like(grad_tile))
        product = (
            jnp.einsum("gqf,gnkf->gqnk", query_head, key_tile, preferred_element_type=jnp.float32)
            * score_scale
        )
        largest = jnp.max(jnp.where(allowed, product, neg_fill), axis=(2, 3), keepdims=True)
        denominator = jnp.sum(
            jnp.where(allowed, jnp.exp(product - largest), 0.0), axis=(2, 3), keepdims=True
        )
        log_total = largest + jnp.log(denominator)
        probability = jnp.where(allowed, jnp.exp(product - log_total), 0.0)
        grad_probs = jnp.einsum(
            "gqf,gnkf->gqnk", grad_head, value_tile, preferred_element_type=jnp.float32
        )
        row_delta = jnp.sum(probability * grad_probs, axis=(2, 3), keepdims=True)
        grad_scores = (probability * (grad_probs - row_delta)).astype(jnp.bfloat16)
        prob_low = probability.astype(jnp.bfloat16)
        query_term = (
            jnp.einsum("gqnk,gnkf->gqf", grad_scores, key_tile, preferred_element_type=jnp.float32)
            * score_scale
        )
        query_sum = query_sum + jnp.where(column_mask, query_term, 0.0)
        key_sum = (
            key_sum
            + jnp.einsum(
                "gqnk,gqf->gnkf", grad_scores, query_head, preferred_element_type=jnp.float32
            )
            * score_scale
        )
        value_sum = value_sum + jnp.einsum(
            "gqnk,gqf->gnkf", prob_low, grad_head, preferred_element_type=jnp.float32
        )
        logs.append(log_total[:, :, 0, 0])
        deltas.append(row_delta[:, :, 0, 0])
    return (query_sum, key_sum, value_sum, jnp.stack(logs, axis=1), jnp.stack(deltas, axis=1))


def per_device(queries, keys_in, values, d_out, token_count, block_ids, neighbours):
    head_count = lax.axis_size("head")
    blk_count = lax.axis_size("blk")
    blk_index = lax.axis_index("blk")
    shard_rows = queries.shape[0]
    block_rows = BLK
    head_width = HD
    score_scale = 1.0 / math.sqrt(head_width)
    query_rows, key_rows, value_rows, grad_rows = (
        lax.all_to_all(queries, "head", split_axis=1, concat_axis=0, tiled=True),
        lax.all_to_all(keys_in, "head", split_axis=1, concat_axis=0, tiled=True),
        lax.all_to_all(values, "head", split_axis=1, concat_axis=0, tiled=True),
        lax.all_to_all(d_out, "head", split_axis=1, concat_axis=0, tiled=True),
    )
    feature_width = query_rows.shape[1]
    masks = head_masks(feature_width, head_width)
    local_blocks = query_rows.shape[0] // block_rows
    key_slots, query_where, key_where = block_tables(
        block_ids, neighbours, blk_count, head_count, block_rows, shard_rows
    )
    token_limit = token_count[0]
    first_slot = blk_index * local_blocks
    my_key_slots = lax.dynamic_slice_in_dim(key_slots, first_slot, local_blocks, 0)
    my_query_where = lax.dynamic_slice_in_dim(query_where, first_slot, local_blocks, 0)
    my_key_where = lax.dynamic_slice_in_dim(key_where, first_slot, local_blocks, 0)
    row_valid = (my_query_where < token_limit).reshape(-1, 1)
    grad_rows = jnp.where(row_valid, grad_rows, jnp.zeros_like(grad_rows))
    query_blocks = query_rows.reshape(local_blocks, block_rows, feature_width)
    grad_blocks = grad_rows.reshape(local_blocks, block_rows, feature_width)
    gathered_keys, gathered_values = (
        lax.all_gather(key_rows, "blk", axis=0, tiled=True),
        lax.all_gather(value_rows, "blk", axis=0, tiled=True),
    )
    key_blocks = gathered_keys.reshape(-1, block_rows, feature_width)
    value_blocks = gathered_values.reshape(-1, block_rows, feature_width)
    group_blocks = group_size(local_blocks, block_rows)
    steps_count = local_blocks // group_blocks

    def local_tiles(start_block):
        query_tile = lax.dynamic_slice_in_dim(query_blocks, start_block, group_blocks, 0)
        grad_tile = lax.dynamic_slice_in_dim(grad_blocks, start_block, group_blocks, 0)
        slot_tile = lax.dynamic_slice_in_dim(my_key_slots, start_block, group_blocks, 0)
        key_tile = jnp.take(key_blocks, slot_tile, axis=0)
        value_tile = jnp.take(value_blocks, slot_tile, axis=0)
        allowed = permitted(
            lax.dynamic_slice_in_dim(my_query_where, start_block, group_blocks, 0),
            lax.dynamic_slice_in_dim(my_key_where, start_block, group_blocks, 0),
            token_limit,
        )
        return (query_tile, grad_tile, slot_tile, key_tile, value_tile, allowed)

    def summed_step(running, step_index):
        query_tile, grad_tile, slot_tile, key_tile, value_tile, allowed = local_tiles(
            step_index * group_blocks
        )
        query_part, key_part, value_part, log_total, row_delta = attend_all(
            query_tile, key_tile, value_tile, grad_tile, allowed, masks, score_scale
        )
        flat_slots = slot_tile.reshape(-1)
        key_sum = running[0].at[flat_slots].add(key_part.reshape(-1, block_rows, feature_width))
        value_sum = running[1].at[flat_slots].add(value_part.reshape(-1, block_rows, feature_width))
        return ((key_sum, value_sum), query_part)

    zero_acc = jnp.zeros((key_blocks.shape[0], block_rows, feature_width), jnp.float32)
    (key_sum, value_sum), query_parts = lax.scan(
        summed_step, (zero_acc, zero_acc), jnp.arange(steps_count, dtype=jnp.int32)
    )
    key_mine, value_mine = (
        lax.psum_scatter(
            key_sum.astype(jnp.bfloat16), "blk", scatter_dimension=0, tiled=True
        ).astype(jnp.float32),
        lax.psum_scatter(
            value_sum.astype(jnp.bfloat16), "blk", scatter_dimension=0, tiled=True
        ).astype(jnp.float32),
    )
    query_grad_rows = query_parts.reshape(local_blocks * block_rows, feature_width).astype(
        jnp.bfloat16
    )
    key_grad_rows = key_mine.reshape(local_blocks * block_rows, feature_width).astype(jnp.bfloat16)
    value_grad_rows = value_mine.reshape(local_blocks * block_rows, feature_width).astype(
        jnp.bfloat16
    )
    gradients = (
        lax.all_to_all(query_grad_rows, "head", split_axis=0, concat_axis=1, tiled=True),
        lax.all_to_all(key_grad_rows, "head", split_axis=0, concat_axis=1, tiled=True),
        lax.all_to_all(value_grad_rows, "head", split_axis=0, concat_axis=1, tiled=True),
    )
    return (gradients[0], gradients[1], gradients[2])


def head_kernel(
    ring,
    blk_count,
    near,
    limit_ref,
    ids_ref,
    nbr_ref,
    q_hbm,
    k_hbm,
    v_hbm,
    g_hbm,
    gq_out,
    gk_out,
    gv_out,
    q_ref,
    k_ref,
    v_ref,
    g_ref,
    qk_send,
    gv_send,
    qk_land,
    gv_land,
    kt_buf,
    key_biased,
    work,
    work_next,
    shrink,
    shrink_row,
    prob_low,
    dscores,
    out_send,
    out_land,
    stored_of,
    slot_of,
    term_at,
    load_sem,
    send_sem,
    recv_sem,
):
    rows = BLK
    width = HD
    scale = 1.0 / math.sqrt(width)
    me = lax.axis_index("head") * blk_count + lax.axis_index("blk")
    limit = limit_ref[0]

    def place(peer):
        return {"head": lax.div(peer, blk_count), "blk": lax.rem(peer, blk_count)}

    def copy_to(kind, source, target, slot, peer):
        return pltpu.make_async_remote_copy(
            src_ref=source,
            dst_ref=target,
            send_sem=send_sem.at[kind, slot],
            recv_sem=recv_sem.at[kind, me],
            device_id=place(peer),
            device_id_type=pl.DeviceIdType.MESH,
        )

    def await_from(kind, target, peer):
        pltpu.make_async_remote_copy(
            src_ref=target,
            dst_ref=target,
            send_sem=send_sem.at[kind, peer],
            recv_sem=recv_sem.at[kind, peer],
            device_id=place(peer),
            device_id_type=pl.DeviceIdType.MESH,
        ).wait_recv()

    def others(body):
        def step(distance, carry):
            body(lax.rem(me + distance, ring))
            return carry

        lax.fori_loop(1, ring, step, 0)

    sources = ((q_hbm, q_ref), (k_hbm, k_ref), (g_hbm, g_ref), (v_hbm, v_ref))
    loads = [
        pltpu.make_async_copy(source, held, load_sem.at[index])
        for index, (source, held) in enumerate(sources)
    ]
    for load in loads:
        load.start()

    barrier = pltpu.get_barrier_semaphore()
    others(
        lambda peer: pl.semaphore_signal(
            barrier, inc=1, device_id=place(peer), device_id_type=pl.DeviceIdType.MESH
        )
    )

    row_index = lax.broadcasted_iota(jnp.int32, (rows, 2 * width), 0)

    for load in loads:
        load.wait()
    my_limit = limit - ids_ref[me] * rows
    for pair in range(ring // 2):
        columns = slice(pair * 2 * width, (pair + 1) * 2 * width)
        q_tile = q_ref[:, columns] * jnp.asarray(scale, jnp.bfloat16)
        k_tile = k_ref[:, columns]
        g_tile = jnp.where(row_index < my_limit, g_ref[:, columns].astype(jnp.float32), 0.0)
        g_tile = g_tile.astype(jnp.bfloat16)
        v_tile = v_ref[:, columns]
        for side in range(2):
            part = slice(side * width, (side + 1) * width)
            qk_send[2 * pair + side] = jnp.concatenate([q_tile[:, part], k_tile[:, part]], axis=1)
            gv_send[2 * pair + side] = jnp.concatenate([g_tile[:, part], v_tile[:, part]], axis=1)

    pl.semaphore_wait(barrier, ring - 1)
    others(lambda peer: copy_to(0, qk_send.at[peer], qk_land.at[me], peer, peer).start())
    qk_land[me] = qk_send[me]
    gv_land[me] = gv_send[me]

    def find_stored(block, carry):
        where = jnp.int32(0)
        for stored in range(ring):
            where = jnp.where(ids_ref[stored] == block, jnp.int32(stored), where)
        stored_of[block] = where
        return carry

    lax.fori_loop(0, ring, find_stored, 0)

    def find_slots(query, carry):
        block = ids_ref[query]
        for entry in range(near):
            slot_of[query * near + entry] = stored_of[nbr_ref[block, entry]]
        return carry

    lax.fori_loop(0, ring, find_slots, 0)

    def find_terms(key, carry):
        def visit(query, state):
            hit = jnp.int32(-1)
            for entry in range(near):
                term = query * near + entry
                hit = jnp.where(slot_of[term] == key, term, hit)
            return tuple(
                jnp.where(hit >= 0, older, held) for older, held in zip((hit,) + state, state)
            )

        state = lax.fori_loop(0, ring, visit, (jnp.int32(0),) * near)
        for rank in range(near):
            term_at[key * near + rank] = state[rank]
        return carry

    lax.fori_loop(0, ring, find_terms, 0)

    others(lambda peer: copy_to(0, qk_send.at[peer], qk_land.at[me], peer, peer).wait_send())
    others(lambda peer: copy_to(1, gv_send.at[peer], gv_land.at[me], peer, peer).start())
    others(lambda peer: await_from(0, qk_land.at[peer], peer))

    lane = lax.broadcasted_iota(jnp.int32, (rows, 2 * width), 1)
    upper = lane >= width

    def turn_keys(block, carry):
        tile = qk_land[block].astype(jnp.float32)
        kt_buf[block] = tile.T[width:, :].astype(jnp.bfloat16)
        real = row_index < limit - ids_ref[block] * rows
        bias = jnp.where((lane == 0) & ~real, neg_fill, 0.0)
        key_biased[block] = jnp.where(upper, tile, bias).astype(jnp.bfloat16)
        return carry

    lax.fori_loop(0, ring, turn_keys, 0)

    nt = (((1,), (1,)), ((), ()))

    def as_upper(tile, lowest):
        wide = tile.astype(jnp.float32)
        moved = jnp.concatenate([wide[:, width:], wide[:, :width]], axis=1)
        return jnp.where(upper, moved, jnp.where(lane == 0, lowest, 0.0)).astype(jnp.bfloat16)

    itself = row_index == lax.broadcasted_iota(jnp.int32, (rows, rows), 1)

    def weigh(query, held):
        block = ids_ref[query]
        own = slot_of[query * near]
        against = as_upper(qk_land[query], 1.0)
        keys = jnp.concatenate(
            [key_biased[slot_of[query * near + entry]] for entry in range(1, near)], axis=0
        )
        first = lax.dot_general(
            qk_land[own], as_upper(qk_land[query], 0.0), nt, preferred_element_type=jnp.float32
        )
        real = row_index < limit - block * rows
        held[:rows] = jnp.where(real | itself, first, neg_fill)
        held[rows:] = lax.dot_general(keys, against, nt, preferred_element_type=jnp.float32)
        largest = jnp.max(held[...], axis=0, keepdims=True)
        grown = jnp.exp(held[...] - largest).astype(jnp.bfloat16)
        total = jnp.sum(grown.astype(jnp.float32), axis=0, keepdims=True)
        prob_low[pl.ds(query * near, near)] = grown.reshape(near, rows, rows)
        shrink[query] = jnp.broadcast_to(1.0 / total, (rows, rows)).T
        shrink_row[query] = jnp.broadcast_to(1.0 / total, (8, rows))

    def weigh_two(step, carry):
        weigh(2 * step, work)
        weigh(2 * step + 1, work_next)
        return carry

    lax.fori_loop(0, ring // 2, weigh_two, 0)

    def hand_out(kind, block, tile):
        out_send[kind, block] = tile

        @pl.when(block != me)
        def _():
            copy_to(
                2 + kind, out_send.at[kind, block], out_land.at[kind, me], block, block
            ).start()

        @pl.when(block == me)
        def _():
            out_land[kind, me] = tile

    def fold(tile):
        return jnp.concatenate([tile[: rows // 2, :width], tile[rows // 2 :, :width]], axis=1)

    def key_terms(weights, tiles, key):
        terms = [term_at[key * near + rank] for rank in range(near)]
        left = jnp.concatenate([weights[term] for term in terms], axis=1)
        right = jnp.concatenate([tiles[lax.div(term, near)] for term in terms], axis=0)
        total = jnp.dot(left, right, preferred_element_type=jnp.float32)
        return fold(total).astype(jnp.bfloat16)

    others(lambda peer: await_from(1, gv_land.at[peer], peer))

    def scale_grads(block, carry):
        tile = gv_land[block].astype(jnp.float32)
        gv_land[block] = jnp.where(upper, tile, tile * shrink[block]).astype(jnp.bfloat16)
        return carry

    lax.fori_loop(0, ring, scale_grads, 0)

    def differentiate(query, held):
        against = as_upper(gv_land[query], 0.0)
        slots = [slot_of[query * near + entry] for entry in range(near)]
        values = jnp.concatenate([gv_land[slot] for slot in slots], axis=0)
        held[...] = lax.dot_general(values, against, nt, preferred_element_type=jnp.float32)
        prob = prob_low[pl.ds(query * near, near)].reshape(near * rows, rows)
        delta = jnp.sum(prob.astype(jnp.float32) * held[...], axis=0, keepdims=True)
        delta = delta * shrink_row[query][:1]
        slope = (prob.astype(jnp.float32) * (held[...] - delta)).astype(jnp.bfloat16)
        dscores[pl.ds(query * near, near)] = slope.reshape(near, rows, rows)
        turned = jnp.concatenate([kt_buf[slot] for slot in slots], axis=1)
        total = jnp.dot(turned, slope, preferred_element_type=jnp.float32) * scale
        return total.astype(jnp.bfloat16)

    def middle(step, carry):
        first = lax.rem(me + 1 + 2 * step, ring)
        second = lax.rem(me + 2 + 2 * step, ring)
        results = (
            (0, first, differentiate(first, work)),
            (2, first, key_terms(prob_low, gv_land, first)),
            (0, second, differentiate(second, work_next)),
            (2, second, key_terms(prob_low, gv_land, second)),
        )
        for result in results:
            hand_out(*result)
        return carry

    lax.fori_loop(0, ring // 2, middle, 0)

    def last(step, carry):
        first = lax.rem(me + 1 + 2 * step, ring)
        second = lax.rem(me + 2 + 2 * step, ring)
        results = (
            (1, first, key_terms(dscores, qk_land, first)),
            (1, second, key_terms(dscores, qk_land, second)),
        )
        for result in results:
            hand_out(*result)
        return carry

    lax.fori_loop(0, ring // 2, last, 0)

    def unfold(kind, out):
        for pair in range(ring // 2):
            columns = slice(pair * 2 * width, (pair + 1) * 2 * width)
            first, second = out_land[kind, 2 * pair], out_land[kind, 2 * pair + 1]
            out[: rows // 2, columns] = jnp.concatenate(
                [first[:, :width], second[:, :width]], axis=1
            )
            out[rows // 2 :, columns] = jnp.concatenate(
                [first[:, width:], second[:, width:]], axis=1
            )

    others(lambda peer: await_from(4, out_land.at[2, peer], peer))
    unfold(2, gv_out)
    others(lambda peer: await_from(2, out_land.at[0, peer], peer))
    for pair in range(ring // 2):
        columns = slice(pair * 2 * width, (pair + 1) * 2 * width)
        tile = jnp.concatenate([out_land[0, 2 * pair], out_land[0, 2 * pair + 1]], axis=0)
        gq_out[:, columns] = tile.astype(jnp.float32).T.astype(jnp.bfloat16)
    others(lambda peer: await_from(3, out_land.at[1, peer], peer))
    unfold(1, gk_out)

    others(lambda peer: copy_to(1, gv_send.at[peer], gv_land.at[me], peer, peer).wait_send())
    for kind in range(3):
        others(
            lambda peer: copy_to(
                2 + kind, out_send.at[kind, peer], out_land.at[kind, me], peer, peer
            ).wait_send()
        )


def per_head_device(
    ring, blk_count, queries, keys_in, values, d_out, token_count, block_ids, neighbours
):
    rows, features = queries.shape
    near = neighbours.shape[1]
    tile = (rows, 2 * HD)
    low = jnp.bfloat16
    smem = pl.BlockSpec(memory_space=pltpu.SMEM)
    vmem = pl.BlockSpec(memory_space=pltpu.VMEM)
    return pl.pallas_call(
        functools.partial(head_kernel, ring, blk_count, near),
        out_shape=[jax.ShapeDtypeStruct((rows, features), low)] * 3,
        in_specs=[smem] * 3 + [pl.BlockSpec(memory_space=pl.ANY)] * 4,
        out_specs=[vmem] * 3,
        scratch_shapes=[pltpu.VMEM((rows, features), low)] * 4
        + [
            pltpu.VMEM((ring,) + tile, low),
            pltpu.VMEM((ring,) + tile, low),
            pltpu.VMEM((ring,) + tile, low),
            pltpu.VMEM((ring,) + tile, low),
            pltpu.VMEM((ring, HD, rows), low),
            pltpu.VMEM((ring,) + tile, low),
            pltpu.VMEM((near * rows, rows), jnp.float32),
            pltpu.VMEM((near * rows, rows), jnp.float32),
            pltpu.VMEM((ring, rows, rows), jnp.float32),
            pltpu.VMEM((ring, 8, rows), jnp.float32),
            pltpu.VMEM((ring * near, rows, rows), low),
            pltpu.VMEM((ring * near, rows, rows), low),
            pltpu.VMEM((3, ring, HD, rows), low),
            pltpu.VMEM((3, ring, HD, rows), low),
            pltpu.SMEM((ring,), jnp.int32),
            pltpu.SMEM((ring * near,), jnp.int32),
            pltpu.SMEM((ring * near,), jnp.int32),
            pltpu.SemaphoreType.DMA((4,)),
            pltpu.SemaphoreType.DMA((5, ring)),
            pltpu.SemaphoreType.DMA((5, ring)),
        ],
        compiler_params=pltpu.CompilerParams(
            collective_id=0, has_side_effects=True, vmem_limit_bytes=60 * 1024 * 1024
        ),
        cost_estimate=pl.CostEstimate(
            flops=10 * ring * near * rows * rows * HD,
            bytes_accessed=14 * rows * features,
            transcendentals=ring * near * rows * rows,
        ),
    )(token_count, block_ids, neighbours, queries, keys_in, values, d_out)


def route(mesh, queries, *rest):
    rows, features = queries.shape
    ring = mesh.shape["head"] * mesh.shape["blk"]
    if rows == BLK and features == ring * HD and 2 * HD == BLK and ring % 2 == 0:
        return tuple(per_head_device(ring, mesh.shape["blk"], queries, *rest))
    return per_device(queries, *rest)


def solution(mesh):
    return jax.shard_map(
        functools.partial(route, mesh),
        mesh=mesh,
        in_specs=(
            P(("bend", "head", "blk"), None),
            P(("bend", "head", "blk"), None),
            P(("bend", "head", "blk"), None),
            P(("bend", "head", "blk"), None),
            P("bend"),
            P("bend"),
            P("bend", None),
        ),
        out_specs=(
            P(("bend", "head", "blk"), None),
            P(("bend", "head", "blk"), None),
            P(("bend", "head", "blk"), None),
        ),
        check_vma=False,
    )
```

```python
import functools
import math

import jax
import jax.numpy as jnp
from jax import lax
from jax.experimental import pallas as pl
from jax.experimental.pallas import tpu as pltpu
from jax.sharding import PartitionSpec as P

HD = 64
BLK = 128


neg_fill = -1e30
row_target = 512


def lookup(entries, wanted):
    matches = wanted[..., None] == jnp.arange(entries.shape[0], dtype=jnp.int32)
    return jnp.sum(jnp.where(matches, entries, 0), axis=-1)


def lookup_rows(entries, wanted):
    matches = wanted[..., None] == jnp.arange(entries.shape[0], dtype=jnp.int32)
    return jnp.sum(jnp.where(matches[..., None], entries, 0), axis=-2)


def group_size(blocks, block_rows):
    target = max(1, min(blocks, row_target // block_rows))
    while blocks % target != 0:
        target = target - 1
    return target


def block_tables(block_ids, neighbours, blk_count, head_count, block_rows, shard_rows):
    per_shard = shard_rows // block_rows
    local_blocks = head_count * per_shard
    slot_ids = jnp.arange(blk_count * local_blocks, dtype=jnp.int32)
    source = slot_ids // local_blocks
    within = slot_ids % local_blocks
    stored = (within // per_shard * blk_count + source) * per_shard + within % per_shard
    global_slot = lookup(block_ids, stored)
    matches = global_slot[None, :] == slot_ids[:, None]
    slot_global = jnp.sum(jnp.where(matches, slot_ids[None, :], 0), axis=1)
    key_global = lookup_rows(neighbours, global_slot)
    key_slots = lookup(slot_global, key_global)
    offsets = jnp.arange(block_rows, dtype=jnp.int32)
    query_where = global_slot[:, None] * block_rows + offsets
    key_where = key_global[:, :, None] * block_rows + offsets
    return (key_slots, query_where, key_where)


def permitted(query_where, key_where, token_limit):
    inside = key_where[:, None] < token_limit
    itself = key_where[:, None] == query_where[:, :, None, None]
    return inside | itself


def head_masks(feature_width, head_width):
    heads_here = feature_width // head_width
    owner_head = jnp.arange(feature_width, dtype=jnp.int32) // head_width
    return owner_head[None, :] == jnp.arange(heads_here, dtype=jnp.int32)[:, None]


def attend_all(query_tile, key_tile, value_tile, grad_tile, allowed, masks, score_scale):
    heads_here = masks.shape[0]
    query_sum = jnp.zeros(query_tile.shape, jnp.float32)
    key_sum = jnp.zeros(key_tile.shape, jnp.float32)
    value_sum = jnp.zeros(key_tile.shape, jnp.float32)
    logs = []
    deltas = []
    for head in range(heads_here):
        column_mask = masks[head]
        query_head = jnp.where(column_mask, query_tile, jnp.zeros_like(query_tile))
        grad_head = jnp.where(column_mask, grad_tile, jnp.zeros_like(grad_tile))
        product = (
            jnp.einsum("gqf,gnkf->gqnk", query_head, key_tile, preferred_element_type=jnp.float32)
            * score_scale
        )
        largest = jnp.max(jnp.where(allowed, product, neg_fill), axis=(2, 3), keepdims=True)
        denominator = jnp.sum(
            jnp.where(allowed, jnp.exp(product - largest), 0.0), axis=(2, 3), keepdims=True
        )
        log_total = largest + jnp.log(denominator)
        probability = jnp.where(allowed, jnp.exp(product - log_total), 0.0)
        grad_probs = jnp.einsum(
            "gqf,gnkf->gqnk", grad_head, value_tile, preferred_element_type=jnp.float32
        )
        row_delta = jnp.sum(probability * grad_probs, axis=(2, 3), keepdims=True)
        grad_scores = (probability * (grad_probs - row_delta)).astype(jnp.bfloat16)
        prob_low = probability.astype(jnp.bfloat16)
        query_term = (
            jnp.einsum("gqnk,gnkf->gqf", grad_scores, key_tile, preferred_element_type=jnp.float32)
            * score_scale
        )
        query_sum = query_sum + jnp.where(column_mask, query_term, 0.0)
        key_sum = (
            key_sum
            + jnp.einsum(
                "gqnk,gqf->gnkf", grad_scores, query_head, preferred_element_type=jnp.float32
            )
            * score_scale
        )
        value_sum = value_sum + jnp.einsum(
            "gqnk,gqf->gnkf", prob_low, grad_head, preferred_element_type=jnp.float32
        )
        logs.append(log_total[:, :, 0, 0])
        deltas.append(row_delta[:, :, 0, 0])
    return (query_sum, key_sum, value_sum, jnp.stack(logs, axis=1), jnp.stack(deltas, axis=1))


def per_device(queries, keys_in, values, d_out, token_count, block_ids, neighbours):
    head_count = lax.axis_size("head")
    blk_count = lax.axis_size("blk")
    blk_index = lax.axis_index("blk")
    shard_rows = queries.shape[0]
    block_rows = BLK
    head_width = HD
    score_scale = 1.0 / math.sqrt(head_width)
    query_rows, key_rows, value_rows, grad_rows = (
        lax.all_to_all(queries, "head", split_axis=1, concat_axis=0, tiled=True),
        lax.all_to_all(keys_in, "head", split_axis=1, concat_axis=0, tiled=True),
        lax.all_to_all(values, "head", split_axis=1, concat_axis=0, tiled=True),
        lax.all_to_all(d_out, "head", split_axis=1, concat_axis=0, tiled=True),
    )
    feature_width = query_rows.shape[1]
    masks = head_masks(feature_width, head_width)
    local_blocks = query_rows.shape[0] // block_rows
    key_slots, query_where, key_where = block_tables(
        block_ids, neighbours, blk_count, head_count, block_rows, shard_rows
    )
    token_limit = token_count[0]
    first_slot = blk_index * local_blocks
    my_key_slots = lax.dynamic_slice_in_dim(key_slots, first_slot, local_blocks, 0)
    my_query_where = lax.dynamic_slice_in_dim(query_where, first_slot, local_blocks, 0)
    my_key_where = lax.dynamic_slice_in_dim(key_where, first_slot, local_blocks, 0)
    row_valid = (my_query_where < token_limit).reshape(-1, 1)
    grad_rows = jnp.where(row_valid, grad_rows, jnp.zeros_like(grad_rows))
    query_blocks = query_rows.reshape(local_blocks, block_rows, feature_width)
    grad_blocks = grad_rows.reshape(local_blocks, block_rows, feature_width)
    gathered_keys, gathered_values = (
        lax.all_gather(key_rows, "blk", axis=0, tiled=True),
        lax.all_gather(value_rows, "blk", axis=0, tiled=True),
    )
    key_blocks = gathered_keys.reshape(-1, block_rows, feature_width)
    value_blocks = gathered_values.reshape(-1, block_rows, feature_width)
    group_blocks = group_size(local_blocks, block_rows)
    steps_count = local_blocks // group_blocks

    def local_tiles(start_block):
        query_tile = lax.dynamic_slice_in_dim(query_blocks, start_block, group_blocks, 0)
        grad_tile = lax.dynamic_slice_in_dim(grad_blocks, start_block, group_blocks, 0)
        slot_tile = lax.dynamic_slice_in_dim(my_key_slots, start_block, group_blocks, 0)
        key_tile = jnp.take(key_blocks, slot_tile, axis=0)
        value_tile = jnp.take(value_blocks, slot_tile, axis=0)
        allowed = permitted(
            lax.dynamic_slice_in_dim(my_query_where, start_block, group_blocks, 0),
            lax.dynamic_slice_in_dim(my_key_where, start_block, group_blocks, 0),
            token_limit,
        )
        return (query_tile, grad_tile, slot_tile, key_tile, value_tile, allowed)

    def summed_step(running, step_index):
        query_tile, grad_tile, slot_tile, key_tile, value_tile, allowed = local_tiles(
            step_index * group_blocks
        )
        query_part, key_part, value_part, log_total, row_delta = attend_all(
            query_tile, key_tile, value_tile, grad_tile, allowed, masks, score_scale
        )
        flat_slots = slot_tile.reshape(-1)
        key_sum = running[0].at[flat_slots].add(key_part.reshape(-1, block_rows, feature_width))
        value_sum = running[1].at[flat_slots].add(value_part.reshape(-1, block_rows, feature_width))
        return ((key_sum, value_sum), query_part)

    zero_acc = jnp.zeros((key_blocks.shape[0], block_rows, feature_width), jnp.float32)
    (key_sum, value_sum), query_parts = lax.scan(
        summed_step, (zero_acc, zero_acc), jnp.arange(steps_count, dtype=jnp.int32)
    )
    key_mine, value_mine = (
        lax.psum_scatter(
            key_sum.astype(jnp.bfloat16), "blk", scatter_dimension=0, tiled=True
        ).astype(jnp.float32),
        lax.psum_scatter(
            value_sum.astype(jnp.bfloat16), "blk", scatter_dimension=0, tiled=True
        ).astype(jnp.float32),
    )
    query_grad_rows = query_parts.reshape(local_blocks * block_rows, feature_width).astype(
        jnp.bfloat16
    )
    key_grad_rows = key_mine.reshape(local_blocks * block_rows, feature_width).astype(jnp.bfloat16)
    value_grad_rows = value_mine.reshape(local_blocks * block_rows, feature_width).astype(
        jnp.bfloat16
    )
    gradients = (
        lax.all_to_all(query_grad_rows, "head", split_axis=0, concat_axis=1, tiled=True),
        lax.all_to_all(key_grad_rows, "head", split_axis=0, concat_axis=1, tiled=True),
        lax.all_to_all(value_grad_rows, "head", split_axis=0, concat_axis=1, tiled=True),
    )
    return (gradients[0], gradients[1], gradients[2])


def head_kernel(
    ring,
    blk_count,
    near,
    limit_ref,
    ids_ref,
    nbr_ref,
    q_hbm,
    k_hbm,
    v_hbm,
    g_hbm,
    gq_out,
    gk_out,
    gv_out,
    q_ref,
    k_ref,
    v_ref,
    g_ref,
    qk_send,
    gv_send,
    qk_land,
    gv_land,
    kt_buf,
    key_biased,
    work,
    work_next,
    work_third,
    work_fourth,
    shrink,
    shrink_row,
    prob_low,
    dscores,
    out_send,
    out_land,
    stored_of,
    slot_of,
    term_at,
    load_sem,
    send_sem,
    recv_sem,
):
    rows = BLK
    width = HD
    scale = 1.0 / math.sqrt(width)
    me = lax.axis_index("head") * blk_count + lax.axis_index("blk")
    limit = limit_ref[0]

    def place(peer):
        return {"head": lax.div(peer, blk_count), "blk": lax.rem(peer, blk_count)}

    def copy_to(kind, source, target, slot, peer):
        return pltpu.make_async_remote_copy(
            src_ref=source,
            dst_ref=target,
            send_sem=send_sem.at[kind, slot],
            recv_sem=recv_sem.at[kind, me],
            device_id=place(peer),
            device_id_type=pl.DeviceIdType.MESH,
        )

    def await_from(kind, target, peer):
        pltpu.make_async_remote_copy(
            src_ref=target,
            dst_ref=target,
            send_sem=send_sem.at[kind, peer],
            recv_sem=recv_sem.at[kind, peer],
            device_id=place(peer),
            device_id_type=pl.DeviceIdType.MESH,
        ).wait_recv()

    def others(body):
        def step(distance, carry):
            body(lax.rem(me + distance, ring))
            return carry

        lax.fori_loop(1, ring, step, 0)

    sources = ((q_hbm, q_ref), (k_hbm, k_ref), (g_hbm, g_ref), (v_hbm, v_ref))
    loads = [
        pltpu.make_async_copy(source, held, load_sem.at[index])
        for index, (source, held) in enumerate(sources)
    ]
    for load in loads:
        load.start()

    barrier = pltpu.get_barrier_semaphore()
    others(
        lambda peer: pl.semaphore_signal(
            barrier, inc=1, device_id=place(peer), device_id_type=pl.DeviceIdType.MESH
        )
    )

    row_index = lax.broadcasted_iota(jnp.int32, (rows, 2 * width), 0)

    for load in loads:
        load.wait()
    my_limit = limit - ids_ref[me] * rows
    for pair in range(ring // 2):
        columns = slice(pair * 2 * width, (pair + 1) * 2 * width)
        q_tile = q_ref[:, columns] * jnp.asarray(scale, jnp.bfloat16)
        k_tile = k_ref[:, columns]
        g_tile = jnp.where(row_index < my_limit, g_ref[:, columns].astype(jnp.float32), 0.0)
        g_tile = g_tile.astype(jnp.bfloat16)
        v_tile = v_ref[:, columns]
        for side in range(2):
            part = slice(side * width, (side + 1) * width)
            qk_send[2 * pair + side] = jnp.concatenate([q_tile[:, part], k_tile[:, part]], axis=1)
            gv_send[2 * pair + side] = jnp.concatenate([g_tile[:, part], v_tile[:, part]], axis=1)

    pl.semaphore_wait(barrier, ring - 1)
    others(lambda peer: copy_to(0, qk_send.at[peer], qk_land.at[me], peer, peer).start())
    others(lambda peer: copy_to(1, gv_send.at[peer], gv_land.at[me], peer, peer).start())
    qk_land[me] = qk_send[me]
    gv_land[me] = gv_send[me]

    def find_stored(block, carry):
        where = jnp.int32(0)
        for stored in range(ring):
            where = jnp.where(ids_ref[stored] == block, jnp.int32(stored), where)
        stored_of[block] = where
        return carry

    lax.fori_loop(0, ring, find_stored, 0)

    def find_slots(query, carry):
        block = ids_ref[query]
        for entry in range(near):
            slot_of[query * near + entry] = stored_of[nbr_ref[block, entry]]
        return carry

    lax.fori_loop(0, ring, find_slots, 0)

    def find_terms(key, carry):
        def visit(query, state):
            hit = jnp.int32(-1)
            for entry in range(near):
                term = query * near + entry
                hit = jnp.where(slot_of[term] == key, term, hit)
            return tuple(
                jnp.where(hit >= 0, older, held) for older, held in zip((hit,) + state, state)
            )

        state = lax.fori_loop(0, ring, visit, (jnp.int32(0),) * near)
        for rank in range(near):
            term_at[key * near + rank] = state[rank]
        return carry

    lax.fori_loop(0, ring, find_terms, 0)

    others(lambda peer: await_from(0, qk_land.at[peer], peer))

    lane = lax.broadcasted_iota(jnp.int32, (rows, 2 * width), 1)
    upper = lane >= width

    def turn_keys(block, carry):
        tile = qk_land[block].astype(jnp.float32)
        kt_buf[block] = tile.T[width:, :].astype(jnp.bfloat16)
        real = row_index < limit - ids_ref[block] * rows
        bias = jnp.where((lane == 0) & ~real, neg_fill, 0.0)
        key_biased[block] = jnp.where(upper, tile, bias).astype(jnp.bfloat16)
        return carry

    lax.fori_loop(0, ring, turn_keys, 0)

    nt = (((1,), (1,)), ((), ()))

    def as_upper(tile, lowest):
        wide = tile.astype(jnp.float32)
        moved = jnp.concatenate([wide[:, width:], wide[:, :width]], axis=1)
        return jnp.where(upper, moved, jnp.where(lane == 0, lowest, 0.0)).astype(jnp.bfloat16)

    itself = row_index == lax.broadcasted_iota(jnp.int32, (rows, rows), 1)

    def weigh(query, held):
        block = ids_ref[query]
        own = slot_of[query * near]
        against = as_upper(qk_land[query], 1.0)
        keys = jnp.concatenate(
            [key_biased[slot_of[query * near + entry]] for entry in range(1, near)], axis=0
        )
        first = lax.dot_general(
            qk_land[own], as_upper(qk_land[query], 0.0), nt, preferred_element_type=jnp.float32
        )
        real = row_index < limit - block * rows
        held[:rows] = jnp.where(real | itself, first, neg_fill)
        held[rows:] = lax.dot_general(keys, against, nt, preferred_element_type=jnp.float32)
        largest = jnp.max(held[...], axis=0, keepdims=True)
        grown = jnp.exp(held[...] - largest).astype(jnp.bfloat16)
        total = jnp.sum(grown.astype(jnp.float32), axis=0, keepdims=True)
        prob_low[pl.ds(query * near, near)] = grown.reshape(near, rows, rows)
        shrink[query] = jnp.broadcast_to(1.0 / total, (rows, rows)).T
        shrink_row[query] = jnp.broadcast_to(1.0 / total, (8, rows))

    buffers = (work, work_next, work_third, work_fourth)
    group = len(buffers)

    def weigh_group(step, carry):
        for index, held in enumerate(buffers):
            weigh(group * step + index, held)
        return carry

    lax.fori_loop(0, ring // group, weigh_group, 0)

    def hand_out(kind, block, tile):
        out_send[kind, block] = tile

        @pl.when(block != me)
        def _():
            copy_to(
                2 + kind, out_send.at[kind, block], out_land.at[kind, me], block, block
            ).start()

        @pl.when(block == me)
        def _():
            out_land[kind, me] = tile

    def fold(tile):
        return jnp.concatenate([tile[: rows // 2, :width], tile[rows // 2 :, :width]], axis=1)

    def key_terms(weights, tiles, key):
        terms = [term_at[key * near + rank] for rank in range(near)]
        left = jnp.concatenate([weights[term] for term in terms], axis=1)
        right = jnp.concatenate([tiles[lax.div(term, near)] for term in terms], axis=0)
        total = jnp.dot(left, right, preferred_element_type=jnp.float32)
        return fold(total).astype(jnp.bfloat16)

    others(lambda peer: await_from(1, gv_land.at[peer], peer))

    def scale_grads(block, carry):
        tile = gv_land[block].astype(jnp.float32)
        gv_land[block] = jnp.where(upper, tile, tile * shrink[block]).astype(jnp.bfloat16)
        return carry

    lax.fori_loop(0, ring, scale_grads, 0)

    def differentiate(query, held):
        against = as_upper(gv_land[query], 0.0)
        slots = [slot_of[query * near + entry] for entry in range(near)]
        values = jnp.concatenate([gv_land[slot] for slot in slots], axis=0)
        held[...] = lax.dot_general(values, against, nt, preferred_element_type=jnp.float32)
        prob = prob_low[pl.ds(query * near, near)].reshape(near * rows, rows)
        delta = jnp.sum(prob.astype(jnp.float32) * held[...], axis=0, keepdims=True)
        delta = delta * shrink_row[query][:1]
        slope = (prob.astype(jnp.float32) * (held[...] - delta)).astype(jnp.bfloat16)
        dscores[pl.ds(query * near, near)] = slope.reshape(near, rows, rows)
        turned = jnp.concatenate([kt_buf[slot] for slot in slots], axis=1)
        total = jnp.dot(turned, slope, preferred_element_type=jnp.float32) * scale
        return total.astype(jnp.bfloat16)

    def middle(step, carry):
        first = lax.rem(me + 1 + 2 * step, ring)
        second = lax.rem(me + 2 + 2 * step, ring)
        results = (
            (0, first, differentiate(first, work)),
            (2, first, key_terms(prob_low, gv_land, first)),
            (0, second, differentiate(second, work_next)),
            (2, second, key_terms(prob_low, gv_land, second)),
        )
        for result in results:
            hand_out(*result)
        return carry

    lax.fori_loop(0, ring // 2, middle, 0)

    def last(step, carry):
        keys = [lax.rem(me + 1 + group * step + index, ring) for index in range(group)]
        results = [key_terms(dscores, qk_land, key) for key in keys]
        for key, result in zip(keys, results):
            hand_out(1, key, result)
        return carry

    lax.fori_loop(0, ring // group, last, 0)

    def unfold(kind, out):
        for pair in range(ring // 2):
            columns = slice(pair * 2 * width, (pair + 1) * 2 * width)
            first, second = out_land[kind, 2 * pair], out_land[kind, 2 * pair + 1]
            out[: rows // 2, columns] = jnp.concatenate(
                [first[:, :width], second[:, :width]], axis=1
            )
            out[rows // 2 :, columns] = jnp.concatenate(
                [first[:, width:], second[:, width:]], axis=1
            )

    others(lambda peer: await_from(4, out_land.at[2, peer], peer))
    unfold(2, gv_out)
    others(lambda peer: await_from(2, out_land.at[0, peer], peer))
    for pair in range(ring // 2):
        columns = slice(pair * 2 * width, (pair + 1) * 2 * width)
        tile = jnp.concatenate([out_land[0, 2 * pair], out_land[0, 2 * pair + 1]], axis=0)
        gq_out[:, columns] = tile.astype(jnp.float32).T.astype(jnp.bfloat16)
    others(lambda peer: await_from(3, out_land.at[1, peer], peer))
    unfold(1, gk_out)

    others(lambda peer: copy_to(0, qk_send.at[peer], qk_land.at[me], peer, peer).wait_send())
    others(lambda peer: copy_to(1, gv_send.at[peer], gv_land.at[me], peer, peer).wait_send())
    for kind in range(3):
        others(
            lambda peer: copy_to(
                2 + kind, out_send.at[kind, peer], out_land.at[kind, me], peer, peer
            ).wait_send()
        )


def per_head_device(
    ring, blk_count, queries, keys_in, values, d_out, token_count, block_ids, neighbours
):
    rows, features = queries.shape
    near = neighbours.shape[1]
    tile = (rows, 2 * HD)
    low = jnp.bfloat16
    smem = pl.BlockSpec(memory_space=pltpu.SMEM)
    vmem = pl.BlockSpec(memory_space=pltpu.VMEM)
    return pl.pallas_call(
        functools.partial(head_kernel, ring, blk_count, near),
        out_shape=[jax.ShapeDtypeStruct((rows, features), low)] * 3,
        in_specs=[smem] * 3 + [pl.BlockSpec(memory_space=pl.ANY)] * 4,
        out_specs=[vmem] * 3,
        scratch_shapes=[pltpu.VMEM((rows, features), low)] * 4
        + [
            pltpu.VMEM((ring,) + tile, low),
            pltpu.VMEM((ring,) + tile, low),
            pltpu.VMEM((ring,) + tile, low),
            pltpu.VMEM((ring,) + tile, low),
            pltpu.VMEM((ring, HD, rows), low),
            pltpu.VMEM((ring,) + tile, low),
            pltpu.VMEM((near * rows, rows), jnp.float32),
            pltpu.VMEM((near * rows, rows), jnp.float32),
            pltpu.VMEM((near * rows, rows), jnp.float32),
            pltpu.VMEM((near * rows, rows), jnp.float32),
            pltpu.VMEM((ring, rows, rows), jnp.float32),
            pltpu.VMEM((ring, 8, rows), jnp.float32),
            pltpu.VMEM((ring * near, rows, rows), low),
            pltpu.VMEM((ring * near, rows, rows), low),
            pltpu.VMEM((3, ring, HD, rows), low),
            pltpu.VMEM((3, ring, HD, rows), low),
            pltpu.SMEM((ring,), jnp.int32),
            pltpu.SMEM((ring * near,), jnp.int32),
            pltpu.SMEM((ring * near,), jnp.int32),
            pltpu.SemaphoreType.DMA((4,)),
            pltpu.SemaphoreType.DMA((5, ring)),
            pltpu.SemaphoreType.DMA((5, ring)),
        ],
        compiler_params=pltpu.CompilerParams(
            collective_id=0, has_side_effects=True, vmem_limit_bytes=60 * 1024 * 1024
        ),
        cost_estimate=pl.CostEstimate(
            flops=10 * ring * near * rows * rows * HD,
            bytes_accessed=14 * rows * features,
            transcendentals=ring * near * rows * rows,
        ),
    )(token_count, block_ids, neighbours, queries, keys_in, values, d_out)


def route(mesh, queries, *rest):
    rows, features = queries.shape
    ring = mesh.shape["head"] * mesh.shape["blk"]
    if rows == BLK and features == ring * HD and 2 * HD == BLK and ring % 4 == 0:
        return tuple(per_head_device(ring, mesh.shape["blk"], queries, *rest))
    return per_device(queries, *rest)


def solution(mesh):
    return jax.shard_map(
        functools.partial(route, mesh),
        mesh=mesh,
        in_specs=(
            P(("bend", "head", "blk"), None),
            P(("bend", "head", "blk"), None),
            P(("bend", "head", "blk"), None),
            P(("bend", "head", "blk"), None),
            P("bend"),
            P("bend"),
            P("bend", None),
        ),
        out_specs=(
            P(("bend", "head", "blk"), None),
            P(("bend", "head", "blk"), None),
            P(("bend", "head", "blk"), None),
        ),
        check_vma=False,
    )
```
